32 devices in a mesh: dp: 2 (over x), seq: 16 (over z, y, core).
Axes of the slice: x: 2, y: 2, z: 4, core: 2. Of those that a mesh axis runs over, the one named last changes fastest.
Arguments:
- hidden_in: bfloat16 [2, 2, 1024, 2048], P(None, 'dp', 'seq'), may hold values from -6 to 6
- cotangent: bfloat16 [2, 2, 1024, 2048], P(None, 'dp', 'seq'), may hold values from -6 to 6
- prefix_len: int32 [2, 2], P(None, 'dp'), may hold values from 102 to 512
- qkv_weight: bfloat16 [6144, 2048], P(('dp', 'seq')), may hold values from -0.125 to 0.125
- dense_weight: bfloat16 [2048, 2048], P(('dp', 'seq')), may hold values from -2 to 2
- fc1_weight: bfloat16 [8192, 2048], P(('dp', 'seq')), may hold values from -0.125 to 0.125
- fc2_weight: bfloat16 [8192, 2048], P(('dp', 'seq')), may hold values from -0.0625 to 0.0625
- norm_gain: bfloat16 [2048], P(('dp', 'seq')), may hold values from 0.5 to 1.5
- norm_shift: bfloat16 [2048], P(('dp', 'seq')), may hold values from -3 to 3
- qkv_bias: bfloat16 [6144], P(('dp', 'seq')), may hold values from -3 to 3
- dense_bias: bfloat16 [2048], P(('dp', 'seq')), may hold values from -3 to 3
- fc1_bias: bfloat16 [8192], P(('dp', 'seq')), may hold values from -3 to 3
- fc2_bias: bfloat16 [2048], P(('dp', 'seq')), may hold values from -3 to 3
Outputs:
- hidden_out: bfloat16 [2, 2, 1024, 2048], P(None, 'dp', 'seq')
- input_grad: float32 [2, 2, 1024, 2048], P(None, 'dp', 'seq')
- qkv_weight_grad: float32 [6144, 2048], P(('dp', 'seq'))
- dense_weight_grad: float32 [2048, 2048], P(('dp', 'seq'))
- fc1_weight_grad: float32 [8192, 2048], P(('dp', 'seq'))
- fc2_weight_grad: float32 [8192, 2048], P(('dp', 'seq'))
- gain_grad: float32 [2048], P(('dp', 'seq'))
- shift_grad: float32 [2048], P(('dp', 'seq'))
- qkv_bias_grad: float32 [6144], P(('dp', 'seq'))
- dense_bias_grad: float32 [2048], P(('dp', 'seq'))
- fc1_bias_grad: float32 [8192], P(('dp', 'seq'))
- fc2_bias_grad: float32 [2048], P(('dp', 'seq'))
The draws below stay inside these ranges and needn't reach their ends.
All inputs are finite; a program needn't handle non-finite values.
Results may differ from the reference program's by a relative error of at most 0.01.
Values may be sent and summed in bfloat16 or wider, within the bound.
A program may use at most 704 MiB of HBM per device.

```python
import math
import jax
import jax.numpy as jnp
from jax import lax

D = 2048
HEADS = 32
HEAD = 64
ROT = 32
FF = 8192
MICRO = 2
LEN = 1024
SEQS = 2


def with_ends(drawn, rng, low, largest):
    spot = [jax.random.randint(jax.random.fold_in(rng, axis), (), 0, length) for axis, length in enumerate(drawn.shape)]
    widest = drawn.shape.index(max(drawn.shape))
    neighbour = spot[:widest] + [(spot[widest] + 1) % drawn.shape[widest]] + spot[widest + 1:]
    return drawn.at[tuple(spot)].set(low).at[tuple(neighbour)].set(largest)


def block_levels(own_key, extent, split, low, largest):
    gain, own = 1.0, jax.random.fold_in(own_key, 6)
    for dim, shards_of in split:
        heights = jnp.exp(jax.random.uniform(jax.random.fold_in(own, dim), (shards_of,), jnp.float32, low / len(split), largest / len(split)))
        gain = gain * jnp.repeat(heights, extent[dim] // shards_of).reshape([-1 if axis == dim else 1 for axis in range(len(extent))])
    return gain


def scatter_about(stream_key, extent, scale, most, split=(), held_as=jnp.bfloat16):
    level = block_levels(stream_key, extent, split, -0.22, 0.18) if split else 1.0
    values = jax.random.normal(stream_key, extent, jnp.float32) * scale * level
    return jnp.minimum(jnp.maximum(values, -most), most).astype(held_as)


def setup_inputs(seed: int = 0) -> dict:
    key_list = jax.random.split(jax.random.key(seed), 14)
    return {
        "hidden_in": scatter_about(key_list[0], (MICRO, SEQS, LEN, D), 1.0, 6.0, ((1, 2), (2, 16))),
        "cotangent": scatter_about(key_list[1], (MICRO, SEQS, LEN, D), 1.0, 6.0, ((1, 2), (2, 16))),
        "prefix_len": with_ends(jax.random.randint(key_list[2], (MICRO, SEQS), LEN // 10, LEN // 2 + 1), jax.random.fold_in(key_list[2], 1), LEN // 10, (LEN // 2 + 1) - 1).astype(jnp.int32),
        "qkv_weight": scatter_about(key_list[3], (3 * D, D), D ** -0.5, 0.125, ((0, 32),)),
        "dense_weight": scatter_about(key_list[4], (D, D), (D * 4 // LEN) ** -0.5, 2.0, ((0, 32),)),
        "fc1_weight": scatter_about(key_list[5], (FF, D), D ** -0.5, 0.125, ((0, 32),)),
        "fc2_weight": scatter_about(key_list[6], (FF, D), FF ** -0.5, 0.0625, ((0, 32),)),
        "norm_gain": jnp.clip(1.0 + 0.1 * jax.random.normal(key_list[7], (D,), jnp.float32), 0.5, 1.5).astype(jnp.bfloat16),
        "norm_shift": scatter_about(key_list[8], (D,), 0.3, 3.0, ((0, 32),)),
        "qkv_bias": scatter_about(key_list[9], (3 * D,), 0.3, 3.0, ((0, 32),)),
        "dense_bias": scatter_about(key_list[10], (D,), 0.3, 3.0, ((0, 32),)),
        "fc1_bias": scatter_about(key_list[11], (FF,), 0.3, 3.0, ((0, 32),)),
        "fc2_bias": scatter_about(key_list[12], (D,), 0.3, 3.0, ((0, 32),)),
    }


NORM_EPS = 1e-05
MASKED_LOW = -1e+30
TANH_FACTOR = 0.7978845608028654
CUBIC_FACTOR = 0.044715

@jax.custom_vjp
def low(v):
    return lax.optimization_barrier(v.astype(jnp.bfloat16)).astype(jnp.float32)

@jax.custom_vjp
def low_back(v):
    return v

def low_keep(v):
    return (low(v), None)

def low_pass(kept, grad):
    return (grad,)

def back_keep(v):
    return (v, None)

def back_low(kept, grad):
    return (low(grad),)
low.defvjp(low_keep, low_pass)
low_back.defvjp(back_keep, back_low)

def gelu_tanh(inputs_in):
    return 0.5 * inputs_in * (1.0 + jnp.tanh(TANH_FACTOR * (inputs_in + CUBIC_FACTOR * inputs_in * inputs_in * inputs_in)))

def rotary_tables(first_place, length):
    half_rot = ROT // 2
    frequency = jnp.power(10000.0, -jnp.arange(half_rot).astype(jnp.float32) * 2.0 / ROT)
    places = (first_place + jnp.arange(length, dtype=jnp.int32)).astype(jnp.float32)
    angles = places[:, None] * frequency[None, :]
    angles = jnp.concatenate([angles, angles], 1)
    return (jnp.cos(angles)[:, None, :], jnp.sin(angles)[:, None, :])

def rotate(head_view, cosine, sine):
    half_rot = ROT // 2
    turned = head_view[..., :ROT]
    swapped = jnp.concatenate([-turned[..., half_rot:], turned[..., :half_rot]], -1)
    return jnp.concatenate([turned * cosine + swapped * sine, head_view[..., ROT:]], -1)

def product(left, right):
    return jnp.dot(left, right, precision=lax.Precision.HIGHEST, preferred_element_type=jnp.float32)

def layer_forward(tokens, limit, weights):
    qkv_weight, dense_weight, fc1_weight, fc2_weight, norm_gain, norm_shift, qkv_bias, dense_bias, fc1_bias, fc2_bias = weights
    length = tokens.shape[0]
    centred = tokens - lax.optimization_barrier(jnp.mean(tokens, 1, keepdims=True))
    rstd = lax.rsqrt(lax.optimization_barrier(jnp.mean(centred * centred, 1, keepdims=True)) + NORM_EPS)
    normed = low(centred * rstd * norm_gain + norm_shift)
    merged = low_back(product(normed, qkv_weight.T) + qkv_bias)
    head_view = merged.reshape(length, 3, HEADS, HEAD)
    cosine, sine = rotary_tables(0, length)
    query = low(rotate(head_view[:, 0], cosine, sine))
    keys = low(rotate(head_view[:, 1], cosine, sine))
    values = low(head_view[:, 2])
    places = jnp.arange(length, dtype=jnp.int32)
    visible = places[None, :] <= jnp.maximum(places[:, None], limit - 1)
    score_scale = 1.0 / math.sqrt(HEAD)

    def one_head(head_parts):
        query_head, key_head, value_head = head_parts
        scores = low_back(product(query_head, key_head.T) * score_scale)
        masked = jnp.where(visible, scores, MASKED_LOW)
        row_top = lax.optimization_barrier(jnp.max(masked, 1, keepdims=True))
        exp_weights = jnp.where(visible, jnp.exp(masked - row_top), 0.0)
        row_total = lax.optimization_barrier(jnp.sum(exp_weights, 1, keepdims=True))
        return product(low(exp_weights), value_head) / row_total
    mixed = lax.map(jax.checkpoint(one_head), (query.transpose(1, 0, 2), keys.transpose(1, 0, 2), values.transpose(1, 0, 2)))
    mixed = low(low_back(mixed.transpose(1, 0, 2).reshape(length, HEADS * HEAD)))
    hidden_pre = low_back(product(normed, fc1_weight.T) + fc1_bias)
    activated = low(gelu_tanh(hidden_pre))
    return tokens + product(mixed, dense_weight) + dense_bias + product(activated, fc2_weight) + fc2_bias

def reference(hidden_in, cotangent, prefix_len, qkv_weight, dense_weight, fc1_weight, fc2_weight, norm_gain, norm_shift, qkv_bias, dense_bias, fc1_bias, fc2_bias):
    weights = tuple((member.astype(jnp.float32) for member in (qkv_weight, dense_weight, fc1_weight, fc2_weight, norm_gain, norm_shift, qkv_bias, dense_bias, fc1_bias, fc2_bias)))
    inputs_all = hidden_in.astype(jnp.float32).reshape(MICRO * SEQS, LEN, D)
    grads_all = cotangent.astype(jnp.float32).reshape(MICRO * SEQS, LEN, D)
    limits = prefix_len.reshape(MICRO * SEQS).astype(jnp.int32)

    def one_sequence(summed, entry):
        tokens, grad_out, limit = entry

        def apply_layer(tokens_in, weights_in):
            return layer_forward(tokens_in, limit, weights_in)
        result, pull_back = jax.vjp(apply_layer, tokens, weights)
        grad_tokens, grad_weights = pull_back(grad_out)
        summed = tuple((old_sum + new_term for old_sum, new_term in zip(summed, grad_weights)))
        return (summed, (result.astype(jnp.bfloat16), grad_tokens))
    zero_sums = tuple((jnp.zeros(member.shape, jnp.float32) for member in weights))
    summed, (outputs, input_grads) = lax.scan(one_sequence, zero_sums, (inputs_all, grads_all, limits))
    return (outputs.reshape(MICRO, SEQS, LEN, D), input_grads.reshape(MICRO, SEQS, LEN, D), summed[0], summed[1], summed[2], summed[3], summed[4], summed[5], summed[6], summed[7], summed[8], summed[9])
```

```python
from functools import partial
import math

import jax
import jax.numpy as jnp
from jax import lax
from jax.experimental import pallas as pl
from jax.experimental.pallas import tpu as pltpu
from jax.sharding import PartitionSpec as P

HEADS = 32
HEAD = 64
ROT = 32


NORM_EPS = 1e-05
MASKED_LOW = -1e30
TANH_FACTOR = 0.7978845608028654
CUBIC_FACTOR = 0.044715


def gelu_tanh(inputs_in):
    return (
        0.5
        * inputs_in
        * (
            1.0
            + jnp.tanh(TANH_FACTOR * (inputs_in + CUBIC_FACTOR * inputs_in * inputs_in * inputs_in))
        )
    )


def rotary_tables(first_place, length):
    half_rot = ROT // 2
    frequency = jnp.power(10000.0, -jnp.arange(half_rot).astype(jnp.float32) * 2.0 / ROT)
    places = (first_place + jnp.arange(length, dtype=jnp.int32)).astype(jnp.float32)
    angles = places[:, None] * frequency[None, :]
    angles = jnp.concatenate([angles, angles], 1)
    return (jnp.cos(angles)[:, None, :], jnp.sin(angles)[:, None, :])


def rotate(head_view, cosine, sine):
    half_rot = ROT // 2
    turned = head_view[..., :ROT]
    swapped = jnp.concatenate([-turned[..., half_rot:], turned[..., :half_rot]], -1)
    return jnp.concatenate([turned * cosine + swapped * sine, head_view[..., ROT:]], -1)


def norm_apply(tokens, scale_gain, shift_bias):
    centred = tokens - jnp.mean(tokens, 1, keepdims=True)
    rstd = lax.rsqrt(jnp.mean(centred * centred, 1, keepdims=True) + NORM_EPS)
    return centred * rstd * scale_gain + shift_bias


def contract_last(left, right):
    return lax.dot_general(
        left, right, (((1,), (1,)), ((), ())), preferred_element_type=jnp.float32
    )


def visible_mask(query_places, key_places, limits):
    reach = jnp.maximum(query_places[None, :], limits[:, None] - 1)
    return (key_places[None, None, :] <= reach[:, :, None])[:, None]


def forward_part(tokens, limits, params, first_place, cosine, sine):
    (
        qkv_weight,
        dense_weight,
        fc1_weight,
        fc2_weight,
        norm_gain,
        norm_shift,
        qkv_bias,
        dense_bias,
        fc1_bias,
        fc2_bias,
    ) = params
    seq_count, local_len, model_width = tokens.shape
    score_scale = 1.0 / math.sqrt(HEAD)
    flat_rows = tokens.reshape(seq_count * local_len, model_width).astype(jnp.float32)
    normed_low = norm_apply(
        flat_rows, norm_gain.astype(jnp.float32), norm_shift.astype(jnp.float32)
    ).astype(jnp.bfloat16)
    merged = contract_last(normed_low, qkv_weight) + qkv_bias.astype(jnp.float32)
    head_view = merged.reshape(seq_count, local_len, 3, HEADS, HEAD)
    query_low = rotate(head_view[:, :, 0], cosine, sine).astype(jnp.bfloat16)
    key_low = (
        rotate(head_view[:, :, 1], cosine, sine)
        .astype(jnp.bfloat16)
        .reshape(seq_count, local_len, model_width)
    )
    value_low = head_view[:, :, 2].astype(jnp.bfloat16).reshape(seq_count, local_len, model_width)
    query_places = first_place + jnp.arange(local_len, dtype=jnp.int32)
    row_top = jnp.full((seq_count, HEADS, local_len), MASKED_LOW, jnp.float32)
    keys_piece = lax.all_gather(key_low, "seq", axis=1, tiled=True)
    values_piece = lax.all_gather(value_low, "seq", axis=1, tiled=True)
    piece_len = keys_piece.shape[1]
    keys_piece = keys_piece.reshape(seq_count, piece_len, HEADS, HEAD)
    values_piece = values_piece.reshape(seq_count, piece_len, HEADS, HEAD)
    scores = (
        jnp.einsum("sqhd,skhd->shqk", query_low, keys_piece, preferred_element_type=jnp.float32)
        * score_scale
    )
    visible = visible_mask(query_places, jnp.arange(piece_len, dtype=jnp.int32), limits)
    masked = jnp.where(visible, scores, MASKED_LOW)
    new_top = jnp.maximum(row_top, jnp.max(masked, -1))
    exp_weights = jnp.where(visible, jnp.exp(masked - new_top[..., None]), 0.0)
    row_total = jnp.sum(exp_weights, -1)
    accum = jnp.einsum(
        "shqk,skhd->shqd",
        exp_weights.astype(jnp.bfloat16),
        values_piece,
        preferred_element_type=jnp.float32,
    )
    row_top, row_total, accum = (new_top, row_total, accum)
    mixed = accum / row_total[..., None]
    log_total = row_top + jnp.log(row_total)
    mixed_low = (
        mixed.transpose(0, 2, 1, 3).reshape(seq_count * local_len, model_width).astype(jnp.bfloat16)
    )
    hidden_pre = contract_last(normed_low, fc1_weight) + fc1_bias.astype(jnp.float32)
    act_low = gelu_tanh(hidden_pre).astype(jnp.bfloat16)
    result = (
        flat_rows
        + jnp.dot(mixed_low, dense_weight, preferred_element_type=jnp.float32)
        + dense_bias.astype(jnp.float32)
    )
    result = (
        result
        + jnp.dot(act_low, fc2_weight, preferred_element_type=jnp.float32)
        + fc2_bias.astype(jnp.float32)
    )
    saved_parts = (
        flat_rows,
        normed_low,
        query_low,
        key_low,
        value_low,
        mixed,
        log_total,
        hidden_pre,
        act_low,
        mixed_low,
    )
    return (result.astype(jnp.bfloat16).reshape(tokens.shape), saved_parts)


def backward_part(grad_low, limits, params, first_place, cosine, sine, saved_parts):
    (
        qkv_weight,
        dense_weight,
        fc1_weight,
        fc2_weight,
        norm_gain,
        norm_shift,
        qkv_bias,
        dense_bias,
        fc1_bias,
        fc2_bias,
    ) = params
    (
        flat_rows,
        normed_low,
        query_low,
        key_low,
        value_low,
        mixed,
        log_total,
        hidden_pre,
        act_low,
        mixed_low,
    ) = saved_parts
    seq_count, local_len, model_width = grad_low.shape
    score_scale = 1.0 / math.sqrt(HEAD)
    grad_rows_low = grad_low.reshape(seq_count * local_len, model_width)
    grad_rows = grad_rows_low.astype(jnp.float32)
    grad_mixed_low = contract_last(grad_rows_low, dense_weight).astype(jnp.bfloat16)
    grad_act = contract_last(grad_rows_low, fc2_weight)
    gelu_pull = jax.vjp(gelu_tanh, hidden_pre)[1]
    grad_hidden_low = gelu_pull(grad_act)[0].astype(jnp.bfloat16)
    grad_out_heads = grad_mixed_low.reshape(seq_count, local_len, HEADS, HEAD)
    delta = jnp.sum(grad_out_heads.astype(jnp.float32).transpose(0, 2, 1, 3) * mixed, -1)
    stats_lse, stats_delta = (
        lax.all_gather(log_total.transpose(0, 2, 1), "seq", axis=1, tiled=True),
        lax.all_gather(delta.transpose(0, 2, 1), "seq", axis=1, tiled=True),
    )
    local_places = first_place + jnp.arange(local_len, dtype=jnp.int32)
    key_heads = key_low.reshape(seq_count, local_len, HEADS, HEAD)
    value_heads = value_low.reshape(seq_count, local_len, HEADS, HEAD)
    keys_piece = lax.all_gather(key_low, "seq", axis=1, tiled=True)
    values_piece = lax.all_gather(value_low, "seq", axis=1, tiled=True)
    piece_len = keys_piece.shape[1]
    keys_piece = keys_piece.reshape(seq_count, piece_len, HEADS, HEAD)
    values_piece = values_piece.reshape(seq_count, piece_len, HEADS, HEAD)
    scores = (
        jnp.einsum("sqhd,skhd->shqk", query_low, keys_piece, preferred_element_type=jnp.float32)
        * score_scale
    )
    visible = visible_mask(local_places, jnp.arange(piece_len, dtype=jnp.int32), limits)
    prob_rows = jnp.where(visible, jnp.exp(scores - log_total[..., None]), 0.0)
    grad_probs = jnp.einsum(
        "sqhd,skhd->shqk", grad_out_heads, values_piece, preferred_element_type=jnp.float32
    )
    grad_scores = (prob_rows * (grad_probs - delta[..., None])).astype(jnp.bfloat16)
    grad_query = score_scale * jnp.einsum(
        "shqk,skhd->sqhd", grad_scores, keys_piece, preferred_element_type=jnp.float32
    )
    query_flat = query_low.reshape(seq_count, local_len, model_width)
    grad_out_flat = grad_mixed_low.reshape(seq_count, local_len, model_width)
    queries_piece = lax.all_gather(query_flat, "seq", axis=1, tiled=True)
    grad_out_piece = lax.all_gather(grad_out_flat, "seq", axis=1, tiled=True)
    piece_len = queries_piece.shape[1]
    queries_piece = queries_piece.reshape(seq_count, piece_len, HEADS, HEAD)
    grad_out_piece = grad_out_piece.reshape(seq_count, piece_len, HEADS, HEAD)
    piece_lse = stats_lse.transpose(0, 2, 1)
    piece_delta = stats_delta.transpose(0, 2, 1)
    scores = (
        jnp.einsum("sqhd,skhd->shqk", queries_piece, key_heads, preferred_element_type=jnp.float32)
        * score_scale
    )
    visible = visible_mask(jnp.arange(piece_len, dtype=jnp.int32), local_places, limits)
    prob_rows = jnp.where(visible, jnp.exp(scores - piece_lse[..., None]), 0.0)
    grad_probs = jnp.einsum(
        "sqhd,skhd->shqk", grad_out_piece, value_heads, preferred_element_type=jnp.float32
    )
    grad_scores = (prob_rows * (grad_probs - piece_delta[..., None])).astype(jnp.bfloat16)
    grad_values = jnp.einsum(
        "shqk,sqhd->skhd",
        prob_rows.astype(jnp.bfloat16),
        grad_out_piece,
        preferred_element_type=jnp.float32,
    )
    grad_keys = score_scale * jnp.einsum(
        "shqk,sqhd->skhd", grad_scores, queries_piece, preferred_element_type=jnp.float32
    )
    grad_keys, grad_values = (grad_keys, grad_values)
    paired = jnp.stack([grad_query, grad_keys], 0)
    rotate_pull = jax.vjp(partial(rotate, cosine=cosine, sine=sine), paired)[1]
    unturned = rotate_pull(paired)[0]
    grad_merged_low = (
        jnp.stack([unturned[0], unturned[1], grad_values], 2)
        .reshape(seq_count * local_len, 3 * model_width)
        .astype(jnp.bfloat16)
    )
    grad_normed = jnp.dot(
        grad_merged_low, qkv_weight, preferred_element_type=jnp.float32
    ) + jnp.dot(grad_hidden_low, fc1_weight, preferred_element_type=jnp.float32)
    norm_pull = jax.vjp(
        norm_apply, flat_rows, norm_gain.astype(jnp.float32), norm_shift.astype(jnp.float32)
    )[1]
    grad_flat, grad_gain, grad_shift = norm_pull(grad_normed)
    input_grad = (grad_rows + grad_flat).reshape(seq_count, local_len, model_width)
    bias_sums = jnp.sum(grad_rows, 0)
    small_terms = (
        grad_gain,
        grad_shift,
        jnp.sum(grad_merged_low.astype(jnp.float32), 0),
        bias_sums,
        jnp.sum(grad_hidden_low.astype(jnp.float32), 0),
        bias_sums,
    )
    operand_set = (normed_low, grad_merged_low, mixed_low, grad_rows_low, grad_hidden_low, act_low)
    return (input_grad, small_terms, operand_set)


def terms_builder(operand_set, row_sizes, model_width, row_count):
    normed_all, grad_merged_all, mixed_all, grad_out_all, grad_hidden_all, act_all = operand_set
    rows_qkv, rows_dense, rows_fc1, rows_fc2 = row_sizes
    block_rows = rows_qkv + rows_dense + rows_fc1 + rows_fc2
    block_count = row_count // block_rows

    def outer_term(left, right, block_width):
        term = lax.dot_general(
            left, right, (((0,), (0,)), ((), ())), preferred_element_type=jnp.float32
        )
        return term.reshape(block_count, block_width, model_width)

    term_parts = [
        outer_term(grad_merged_all, normed_all, rows_qkv),
        outer_term(mixed_all, grad_out_all, rows_dense),
        outer_term(grad_hidden_all, normed_all, rows_fc1),
        outer_term(act_all, grad_out_all, rows_fc2),
    ]
    return jnp.concatenate(term_parts, 1).reshape(row_count, model_width)


def on_device(
    hidden_in,
    cotangent,
    prefix_len,
    qkv_weight,
    dense_weight,
    fc1_weight,
    fc2_weight,
    norm_gain,
    norm_shift,
    qkv_bias,
    dense_bias,
    fc1_bias,
    fc2_bias,
):
    micro_count, seq_count, local_len, model_width = hidden_in.shape
    first_place = lax.axis_index("seq") * local_len
    cosine, sine = rotary_tables(first_place, local_len)
    row_sizes = (
        qkv_weight.shape[0],
        dense_weight.shape[0],
        fc1_weight.shape[0],
        fc2_weight.shape[0],
    )
    block_rows = row_sizes[0] + row_sizes[1] + row_sizes[2] + row_sizes[3]
    params = (
        lax.all_gather(qkv_weight, ("dp", "seq"), axis=0, tiled=True),
        lax.all_gather(dense_weight, ("dp", "seq"), axis=0, tiled=True),
        lax.all_gather(fc1_weight, ("dp", "seq"), axis=0, tiled=True),
        lax.all_gather(fc2_weight, ("dp", "seq"), axis=0, tiled=True),
        lax.all_gather(norm_gain, ("dp", "seq"), axis=0, tiled=True),
        lax.all_gather(norm_shift, ("dp", "seq"), axis=0, tiled=True),
        lax.all_gather(qkv_bias, ("dp", "seq"), axis=0, tiled=True),
        lax.all_gather(dense_bias, ("dp", "seq"), axis=0, tiled=True),
        lax.all_gather(fc1_bias, ("dp", "seq"), axis=0, tiled=True),
        lax.all_gather(fc2_bias, ("dp", "seq"), axis=0, tiled=True),
    )
    outputs = []
    input_grads = []
    small_totals = None
    operand_lists = []
    weight_rows = None
    for batch_index in range(micro_count):
        limits = prefix_len[batch_index]
        result, saved_parts = forward_part(
            hidden_in[batch_index], limits, params, first_place, cosine, sine
        )
        input_grad, small_terms, operand_set = backward_part(
            cotangent[batch_index], limits, params, first_place, cosine, sine, saved_parts
        )
        outputs.append(result)
        input_grads.append(input_grad)
        operand_lists.append(operand_set)
        if small_totals is None:
            small_totals = small_terms
        else:
            small_totals = tuple(
                (old_sum + new_term for old_sum, new_term in zip(small_totals, small_terms))
            )
    joined_set = tuple(
        (jnp.concatenate([entry[place] for entry in operand_lists], 0) for place in range(6))
    )
    weight_rows = lax.psum_scatter(
        terms_builder(
            joined_set, row_sizes, model_width, block_rows * lax.axis_size(("dp", "seq"))
        ),
        ("dp", "seq"),
        scatter_dimension=0,
        tiled=True,
    )
    rows_qkv, rows_dense, rows_fc1, rows_fc2 = row_sizes
    qkv_grad = weight_rows[:rows_qkv]
    dense_grad = weight_rows[rows_qkv : rows_qkv + rows_dense]
    fc1_grad = weight_rows[rows_qkv + rows_dense : rows_qkv + rows_dense + rows_fc1]
    fc2_grad = weight_rows[rows_qkv + rows_dense + rows_fc1 :]
    gain_grad, shift_grad, qkv_bias_grad, dense_bias_grad, fc1_bias_grad, fc2_bias_grad = (
        lax.psum_scatter(small_totals[0], ("dp", "seq"), scatter_dimension=0, tiled=True),
        lax.psum_scatter(small_totals[1], ("dp", "seq"), scatter_dimension=0, tiled=True),
        lax.psum_scatter(small_totals[2], ("dp", "seq"), scatter_dimension=0, tiled=True),
        lax.psum_scatter(small_totals[3], ("dp", "seq"), scatter_dimension=0, tiled=True),
        lax.psum_scatter(small_totals[4], ("dp", "seq"), scatter_dimension=0, tiled=True),
        lax.psum_scatter(small_totals[5], ("dp", "seq"), scatter_dimension=0, tiled=True),
    )
    return (
        jnp.stack(outputs, 0),
        jnp.stack(input_grads, 0),
        qkv_grad,
        dense_grad,
        fc1_grad,
        fc2_grad,
        gain_grad,
        shift_grad,
        qkv_bias_grad,
        dense_bias_grad,
        fc1_bias_grad,
        fc2_bias_grad,
    )


MESH = pl.DeviceIdType.MESH
BF = jnp.bfloat16
F32 = jnp.float32


def place():
    d = lax.axis_index("dp")
    s = lax.axis_index("seq")
    return d, s, s // 4, (s // 2) % 2, s % 2


def seq_of(z, y, c):
    return z * 4 + y * 2 + c


def send(src, dst, ssem, rsem, target):
    copy = pltpu.make_async_remote_copy(
        src_ref=src, dst_ref=dst, send_sem=ssem, recv_sem=rsem, device_id=target, device_id_type=MESH
    )
    copy.start()
    return copy


def await_bytes(ref, sem):
    pltpu.make_async_copy(ref, ref, sem).wait()


def greet_all():
    d, s, z, y, c = place()
    barrier = pltpu.get_barrier_semaphore()

    def greet(k, carry):
        other = lax.rem(d * 16 + s + k, 32)
        pl.semaphore_signal(barrier, inc=1, device_id=(other // 16, other % 16), device_id_type=MESH)
        return carry

    lax.fori_loop(1, 32, greet, 0)
    pl.semaphore_wait(barrier, 31)


class Gather:
    def __init__(self, src, G, local, zs, zr, ys, yr, cs, cr):
        self.src, self.G = src, G
        self.local, self.zs, self.zr, self.ys, self.yr, self.cs, self.cr = local, zs, zr, ys, yr, cs, cr
        self.sent = []

    def start(self):
        d, s, z, y, c = place()
        self.own = pltpu.make_async_copy(self.src, self.G.at[z, y, c], self.local)
        self.own.start()
        dst = self.G.at[z, y, c]
        for dz in (1, 2, 3):
            self.sent.append(
                send(self.src, dst, self.zs.at[dz - 1], self.zr.at[dz - 1], (d, seq_of((z + dz) % 4, y, c)))
            )
        self.sent.append(send(self.src, dst, self.ys.at[0], self.yr.at[0], (d, seq_of(z, 1 - y, c))))

    def across_y(self):
        d, s, z, y, c = place()
        for dz in (1, 2, 3):
            slot = self.G.at[(z + 4 - dz) % 4, y, c]
            await_bytes(slot, self.zr.at[dz - 1])
            self.sent.append(send(slot, slot, self.ys.at[dz], self.yr.at[dz], (d, seq_of(z, 1 - y, c))))
        self.own.wait()
        line = self.G.at[:, y, c]
        self.sent.append(send(line, line, self.cs.at[0], self.cr.at[0], (d, seq_of(z, y, 1 - c))))

    def across_core(self):
        d, s, z, y, c = place()
        for dz in (0, 1, 2, 3):
            await_bytes(self.G.at[(z + 4 - dz) % 4, 1 - y, c], self.yr.at[dz])
        line = self.G.at[:, 1 - y, c]
        self.sent.append(send(line, line, self.cs.at[1], self.cr.at[1], (d, seq_of(z, y, 1 - c))))

    def finish(self):
        d, s, z, y, c = place()
        await_bytes(self.G.at[:, y, 1 - c], self.cr.at[0])
        await_bytes(self.G.at[:, 1 - y, 1 - c], self.cr.at[1])
        for copy in self.sent:
            copy.wait_send()


class Scatter:
    def __init__(self, P, RC, RY, RZ, cs, cr, ys, yr, zs, zr):
        self.P, self.RC, self.RY, self.RZ = P, RC, RY, RZ
        self.cs, self.cr, self.ys, self.yr, self.zs, self.zr = cs, cr, ys, yr, zs, zr
        self.sent = []

    def start(self):
        d, s, z, y, c = place()
        for k, row in ((0, 1 - y), (1, y)):
            self.sent.append(
                send(
                    self.P.at[:, row, 1 - c], self.RC.at[:, row], self.cs.at[k], self.cr.at[k], (d, seq_of(z, y, 1 - c))
                )
            )

    def across_y(self):
        d, s, z, y, c = place()
        await_bytes(self.RC.at[:, 1 - y], self.cr.at[0])
        for dz in (1, 2, 3, 0):
            zz = (z + dz) % 4
            chunk = self.P.at[zz, 1 - y, c]
            chunk[...] = (chunk[...].astype(F32) + self.RC[zz, 1 - y].astype(F32)).astype(BF)
            self.sent.append(
                send(chunk, self.RY.at[zz], self.ys.at[dz], self.yr.at[dz], (d, seq_of(z, 1 - y, c)))
            )

    def across_z(self):
        d, s, z, y, c = place()
        await_bytes(self.RC.at[:, y], self.cr.at[1])
        for dz in (1, 2, 3):
            zz = (z + dz) % 4
            await_bytes(self.RY.at[zz], self.yr.at[dz])
            chunk = self.P.at[zz, y, c]
            chunk[...] = (
                chunk[...].astype(F32) + self.RC[zz, y].astype(F32) + self.RY[zz].astype(F32)
            ).astype(BF)
            self.sent.append(
                send(chunk, self.RZ.at[dz - 1], self.zs.at[dz - 1], self.zr.at[dz - 1], (d, seq_of(zz, y, c)))
            )

    def finish(self):
        d, s, z, y, c = place()
        await_bytes(self.RY.at[z], self.yr.at[0])
        total = self.P[z, y, c].astype(F32) + self.RC[z, y].astype(F32) + self.RY[z].astype(F32)
        for k in (0, 1, 2):
            await_bytes(self.RZ.at[k], self.zr.at[k])
            total = total + self.RZ[k].astype(F32)
        for copy in self.sent:
            copy.wait_send()
        return total


def gather_kernel(
    x_ref, dy_ref, wq_ref, wd_ref, w1_ref, w2_ref,
    N, DY, Wq, Wd, W1, W2,
    local, zs, zr, ys, yr, cs, cr, qs, qr, qxs, qxr, ws, wr, wl,
):
    d, s, z, y, c = place()
    greet_all()
    jobs = []
    for t, (src, G) in enumerate(((x_ref, N), (dy_ref, DY))):
        for m in range(2):
            jobs.append(
                Gather(src.at[m], G.at[m], local.at[t, m], zs.at[t, m], zr.at[t, m], ys.at[t, m], yr.at[t, m], cs.at[t, m], cr.at[t, m])
            )
    jobs[0].start()
    me = d * 16 + s
    for i in range(3):
        b = me * 3 + i
        target, entry = b % 16, b // 16

        @pl.when(target == s)
        def _():
            pltpu.make_async_copy(wq_ref.at[i], Wq.at[entry], qr.at[entry]).start()

        @pl.when(target != s)
        def _():
            send(wq_ref.at[i], Wq.at[entry], qs.at[i], qr.at[entry], (d, target))

    partner = (1 - d, s)
    moved = []
    for k, (src, dst) in enumerate(((w1_ref, W1), (w2_ref, W2), (wd_ref, Wd))):
        own = pltpu.make_async_copy(src, dst.at[d], wl.at[k])
        own.start()
        moved.append((own, send(src, dst.at[d], ws.at[k], wr.at[k], partner)))
    jobs[1].start()
    jobs[2].start()
    jobs[3].start()
    for i in range(3):
        entry = 3 * d + i
        await_bytes(Wq.at[entry], qr.at[entry])
    mine = Wq.at[pl.ds(3 * d, 3)]
    qx = send(mine, mine, qxs.at[0], qxr.at[0], partner)
    for job in jobs:
        job.across_y()
    for job in jobs:
        job.across_core()
    for job in jobs:
        job.finish()
    for k, (own, copy) in enumerate(moved):
        own.wait()
        copy.wait()
    qx.wait()
    for i in range(3):
        target = (me * 3 + i) % 16

        @pl.when(target != s)
        def _():
            await_bytes(wq_ref.at[i], qs.at[i])


def run_gather(x, dy, wq, wd, w1, w2):
    width = x.shape[-1]
    anyspace = pl.BlockSpec(memory_space=pl.ANY)
    dma = pltpu.SemaphoreType.DMA
    return pl.pallas_call(
        gather_kernel,
        name="gather_all",
        out_shape=(
            jax.ShapeDtypeStruct((2, 4, 2, 2, 64, width), BF),
            jax.ShapeDtypeStruct((2, 4, 2, 2, 64, width), BF),
            jax.ShapeDtypeStruct((6, 64, width), BF),
            jax.ShapeDtypeStruct((2, 64, width), BF),
            jax.ShapeDtypeStruct((2, 256, width), BF),
            jax.ShapeDtypeStruct((2, 256, width), BF),
        ),
        in_specs=[anyspace] * 6,
        out_specs=(anyspace,) * 6,
        scratch_shapes=[
            dma((2, 2)), dma((2, 2, 3)), dma((2, 2, 3)), dma((2, 2, 4)), dma((2, 2, 4)), dma((2, 2, 2)), dma((2, 2, 2)),
            dma((3,)), dma((6,)), dma((1,)), dma((1,)), dma((3,)), dma((3,)), dma((3,)),
        ],
        compiler_params=pltpu.CompilerParams(collective_id=0, has_side_effects=True),
    )(x, dy, wq.reshape(3, 64, width), wd, w1, w2)


def scatter_kernel(
    po_ref, pg_ref, gq_ref, gx_ref, O, GN, RX, RQ,
    P, RC, RY, RZ, SQ, XB, load, cs, cr, ys, yr, zs, zr, xs, xr, qs, qr,
):
    d, s, z, y, c = place()
    loads = []
    for t, src in enumerate((po_ref, pg_ref)):
        for m in range(2):
            copy = pltpu.make_async_copy(src.at[m], P.at[t, m], load.at[t, m])
            copy.start()
            loads.append(copy)
    greet_all()
    partner = (1 - d, s)
    xq = send(gq_ref.at[pl.ds(3 * (1 - d), 3)], XB, xs.at[0], xr.at[0], partner)
    xo = send(gx_ref, RX, xs.at[1], xr.at[1], partner)
    jobs = []
    for t in range(2):
        for m in range(2):
            jobs.append(
                Scatter(P.at[t, m], RC.at[t, m], RY.at[t, m], RZ.at[t, m],
                        cs.at[t, m], cr.at[t, m], ys.at[t, m], yr.at[t, m], zs.at[t, m], zr.at[t, m])
            )
    for load_copy, job in zip(loads, jobs):
        load_copy.wait()
        job.start()
    for job in jobs:
        job.across_y()
    for job in jobs:
        job.across_z()
    xq.wait_recv()
    keep = pltpu.make_async_copy(gq_ref.at[pl.ds(3 * d, 3)], SQ, load.at[0, 0])
    keep.start()
    keep.wait()
    for i in range(3):
        SQ[i] = (SQ[i].astype(F32) + XB[i].astype(F32)).astype(BF)
        b = s + 16 * (3 * d + i)
        owner = b // 3 - 16 * d
        where = b % 3

        @pl.when(owner == s)
        def _():
            pltpu.make_async_copy(SQ.at[i], RQ.at[where], qr.at[where]).start()

        @pl.when(owner != s)
        def _():
            send(SQ.at[i], RQ.at[where], qs.at[i], qr.at[where], (d, owner))

    for k, job in enumerate(jobs):
        total = job.finish()
        if k < 2:
            O[k] = total
        else:
            GN[k - 2] = total
    for i in range(3):
        await_bytes(RQ.at[i], qr.at[i])
        b = s + 16 * (3 * d + i)
        owner = b // 3 - 16 * d

        @pl.when(owner != s)
        def _():
            await_bytes(SQ.at[i], qs.at[i])

    xq.wait_send()
    xo.wait()


def run_scatter(po, pg, gq, gx):
    width = po.shape[-1]
    vm = pl.BlockSpec(memory_space=pltpu.VMEM)
    anyspace = pl.BlockSpec(memory_space=pl.ANY)
    dma = pltpu.SemaphoreType.DMA
    return pl.pallas_call(
        scatter_kernel,
        name="scatter_all",
        out_shape=(
            jax.ShapeDtypeStruct((2, 64, width), F32),
            jax.ShapeDtypeStruct((2, 64, width), F32),
            jax.ShapeDtypeStruct(gx.shape, BF),
            jax.ShapeDtypeStruct((3, 64, width), BF),
        ),
        in_specs=[anyspace] * 4,
        out_specs=(vm, vm, anyspace, anyspace),
        scratch_shapes=[
            pltpu.VMEM((2, 2, 4, 2, 2, 64, width), BF),
            pltpu.VMEM((2, 2, 4, 2, 64, width), BF),
            pltpu.VMEM((2, 2, 4, 64, width), BF),
            pltpu.VMEM((2, 2, 3, 64, width), BF),
            pltpu.VMEM((3, 64, width), BF),
            pltpu.VMEM((3, 64, width), BF),
            dma((2, 2)), dma((2, 2, 2)), dma((2, 2, 2)), dma((2, 2, 4)), dma((2, 2, 4)), dma((2, 2, 3)), dma((2, 2, 3)),
            dma((2,)), dma((2,)), dma((3,)), dma((3,)),
        ],
        compiler_params=pltpu.CompilerParams(
            collective_id=1, has_side_effects=True, vmem_limit_bytes=60 * 2**20
        ),
    )(po, pg, gq, gx)


def outer(left, right):
    return lax.dot_general(left, right, (((0,), (0,)), ((), ())), preferred_element_type=F32)


def by_heads(
    hidden_in, cotangent, prefix_len, qkv_weight, dense_weight, fc1_weight, fc2_weight,
    norm_gain, norm_shift, qkv_bias, dense_bias, fc1_bias, fc2_bias,
):
    width = hidden_in.shape[-1]
    length = hidden_in.shape[2] * 16
    d, s, z, y, c = place()
    small = jnp.concatenate([norm_gain, norm_shift, dense_bias, fc2_bias, qkv_bias, fc1_bias])
    small = lax.all_gather(small, ("dp", "seq"), axis=0).astype(F32)
    gain, shift, dense_add, fc2_add = (small[:, 64 * i : 64 * i + 64].reshape(-1) for i in range(4))
    qkv_blocks = small[:, 256:448].reshape(96, 64)
    qkv_add = jnp.take(qkv_blocks, s + 16 * jnp.arange(6), axis=0).reshape(3, 128)
    fc1_blocks = small[:, 448:704]
    fc1_add = jnp.take(fc1_blocks, s + 16 * jnp.arange(2), axis=0).reshape(512)

    rows = hidden_in.reshape(128, width).astype(F32)
    centred = rows - jnp.mean(rows, 1, keepdims=True)
    rstd = lax.rsqrt(jnp.mean(centred * centred, 1, keepdims=True) + NORM_EPS)
    xhat = centred * rstd
    normed = (xhat * gain + shift).astype(BF)

    N, DY, Wq, Wd, W1, W2 = run_gather(
        normed.reshape(2, 64, width), cotangent.reshape(2, 64, width), qkv_weight, dense_weight, fc1_weight, fc2_weight
    )
    Nf = N.reshape(2, length, width)
    DYf = DY.reshape(2, length, width)
    Wq = Wq.reshape(384, width)
    Wd = Wd.reshape(128, width)
    W1 = W1.reshape(512, width)
    W2 = W2.reshape(512, width)
    cosine, sine = rotary_tables(0, length)
    scale = 1.0 / math.sqrt(HEAD)
    po, pg, gms, ghs, acts, mixes = [], [], [], [], [], []
    for m in range(2):
        merged = (contract_last(Nf[m], Wq) + qkv_add.reshape(384)).reshape(length, 3, 2, HEAD)
        query = rotate(merged[:, 0], cosine, sine).astype(BF)
        key = rotate(merged[:, 1], cosine, sine).astype(BF)
        value = merged[:, 2].astype(BF)
        scores = jnp.einsum("qhd,khd->hqk", query, key, preferred_element_type=F32) * scale
        places = jnp.arange(length, dtype=jnp.int32)
        visible = (places[None, :] <= jnp.maximum(places[:, None], prefix_len[m, 0] - 1))[None]
        masked = jnp.where(visible, scores, MASKED_LOW)
        top = jnp.max(masked, -1, keepdims=True)
        weights = jnp.where(visible, jnp.exp(masked - top), 0.0)
        total = jnp.sum(weights, -1, keepdims=True)
        mixed = jnp.einsum("hqk,khd->hqd", weights.astype(BF), value, preferred_element_type=F32) / total
        probs = weights / total
        mixed_low = mixed.transpose(1, 0, 2).reshape(length, 128).astype(BF)
        pre = contract_last(Nf[m], W1) + fc1_add
        act = gelu_tanh(pre).astype(BF)
        po.append(
            (
                jnp.dot(mixed_low, Wd, preferred_element_type=F32) + jnp.dot(act, W2, preferred_element_type=F32)
            ).astype(BF)
        )
        grad_mixed = contract_last(DYf[m], Wd).astype(BF)
        grad_act = contract_last(DYf[m], W2)
        grad_hidden = jax.vjp(gelu_tanh, pre)[1](grad_act)[0].astype(BF)
        gm_heads = grad_mixed.reshape(length, 2, HEAD)
        delta = jnp.sum(gm_heads.astype(F32).transpose(1, 0, 2) * mixed, -1, keepdims=True)
        grad_probs = jnp.einsum("qhd,khd->hqk", gm_heads, value, preferred_element_type=F32)
        grad_scores = (probs * (grad_probs - delta)).astype(BF)
        grad_query = scale * jnp.einsum("hqk,khd->qhd", grad_scores, key, preferred_element_type=F32)
        grad_key = scale * jnp.einsum("hqk,qhd->khd", grad_scores, query, preferred_element_type=F32)
        grad_value = jnp.einsum("hqk,qhd->khd", probs.astype(BF), gm_heads, preferred_element_type=F32)
        pull = jax.vjp(partial(rotate, cosine=cosine, sine=sine), grad_query)[1]
        grad_merged = jnp.stack([pull(grad_query)[0], pull(grad_key)[0], grad_value], 1)
        grad_merged = grad_merged.reshape(length, 384).astype(BF)
        pg.append(
            (
                jnp.dot(grad_merged, Wq, preferred_element_type=F32)
                + jnp.dot(grad_hidden, W1, preferred_element_type=F32)
            ).astype(BF)
        )
        gms.append(grad_merged)
        ghs.append(grad_hidden)
        acts.append(act)
        mixes.append(mixed_low)
    Nall, DYall = Nf.reshape(2 * length, width), DYf.reshape(2 * length, width)
    gm, gh, act, mixed_low = (jnp.concatenate(p, 0) for p in (gms, ghs, acts, mixes))
    gq = outer(gm, Nall)
    gd = outer(mixed_low, DYall).reshape(2, 64, width)
    g1 = outer(gh, Nall).reshape(2, 256, width)
    g2 = outer(act, DYall).reshape(2, 256, width)

    def pick(pair, which):
        return lax.dynamic_index_in_dim(pair, which, 0, False)

    gx = jnp.concatenate([pick(gd, 1 - d), pick(g1, 1 - d), pick(g2, 1 - d)], 0).astype(BF)
    chunks = (2, 4, 2, 2, 64, width)
    O, GN, RX, RQ = run_scatter(
        jnp.stack(po).reshape(chunks), jnp.stack(pg).reshape(chunks), gq.astype(BF).reshape(6, 64, width), gx
    )
    RX = RX.astype(F32)
    hidden_out = (rows.reshape(2, 64, width) + O + (dense_add + fc2_add)).astype(BF)
    dense_grad = pick(gd, d) + RX[:64]
    fc1_grad = pick(g1, d) + RX[64:320]
    fc2_grad = pick(g2, d) + RX[320:]
    qkv_grad = RQ.astype(F32).reshape(192, width)
    grad_normed = GN.reshape(128, width)
    g = grad_normed * gain
    input_grad = cotangent.reshape(128, width).astype(F32) + rstd * (
        g - jnp.mean(g, 1, keepdims=True) - xhat * jnp.mean(g * xhat, 1, keepdims=True)
    )
    gain_sum = jnp.sum(grad_normed * xhat, 0).reshape(32, 64)
    shift_sum = jnp.sum(grad_normed, 0).reshape(32, 64)
    dy_sum = jnp.sum(cotangent.reshape(128, width).astype(F32), 0).reshape(32, 64)
    qb = jnp.zeros((96, 64), F32).at[s + 16 * jnp.arange(6)].set(jnp.sum(gm.astype(F32), 0).reshape(6, 64))
    fb = jnp.zeros((32, 256), F32).at[s + 16 * jnp.arange(2)].set(jnp.sum(gh.astype(F32), 0).reshape(2, 256))
    packed = jnp.concatenate([gain_sum, shift_sum, dy_sum, qb.reshape(32, 192), fb], 1)
    packed = lax.psum_scatter(packed, ("dp", "seq"), scatter_dimension=0, tiled=True)[0]
    return (
        hidden_out.reshape(hidden_in.shape),
        input_grad.reshape(hidden_in.shape),
        qkv_grad,
        dense_grad,
        fc1_grad,
        fc2_grad,
        packed[:64],
        packed[64:128],
        packed[192:384],
        packed[128:192],
        packed[384:640],
        packed[128:192],
    )


def solution(mesh):
    in_specs = (
        P(None, "dp", "seq", None),
        P(None, "dp", "seq", None),
        P(None, "dp"),
        P(("dp", "seq"), None),
        P(("dp", "seq"), None),
        P(("dp", "seq"), None),
        P(("dp", "seq"), None),
        P(("dp", "seq")),
        P(("dp", "seq")),
        P(("dp", "seq")),
        P(("dp", "seq")),
        P(("dp", "seq")),
        P(("dp", "seq")),
    )
    out_specs = (
        P(None, "dp", "seq", None),
        P(None, "dp", "seq", None),
        P(("dp", "seq"), None),
        P(("dp", "seq"), None),
        P(("dp", "seq"), None),
        P(("dp", "seq"), None),
        P(("dp", "seq")),
        P(("dp", "seq")),
        P(("dp", "seq")),
        P(("dp", "seq")),
        P(("dp", "seq")),
        P(("dp", "seq")),
    )
    fits = mesh.shape["dp"] == 2 and mesh.shape["seq"] == 16

    def body(*args):
        return (by_heads if fits and args[0].shape[0] == 2 and args[0].shape[2] == 64 else on_device)(*args)

    return jax.shard_map(
        body, mesh=mesh, in_specs=in_specs, out_specs=out_specs, check_vma=False
    )
```

```python
from functools import partial
import math
from types import SimpleNamespace

import jax
import jax.numpy as jnp
import numpy as np
from jax import lax
from jax.experimental import pallas as pl
from jax.experimental.pallas import tpu as pltpu
from jax.sharding import PartitionSpec as P

HEADS = 32
HEAD = 64
ROT = 32


NORM_EPS = 1e-05
MASKED_LOW = -1e30
TANH_FACTOR = 0.7978845608028654
CUBIC_FACTOR = 0.044715


def gelu_tanh(inputs_in):
    return (
        0.5
        * inputs_in
        * (
            1.0
            + jnp.tanh(TANH_FACTOR * (inputs_in + CUBIC_FACTOR * inputs_in * inputs_in * inputs_in))
        )
    )


def rotary_tables(first_place, length):
    half_rot = ROT // 2
    frequency = jnp.power(10000.0, -jnp.arange(half_rot).astype(jnp.float32) * 2.0 / ROT)
    places = (first_place + jnp.arange(length, dtype=jnp.int32)).astype(jnp.float32)
    angles = places[:, None] * frequency[None, :]
    angles = jnp.concatenate([angles, angles], 1)
    return (jnp.cos(angles)[:, None, :], jnp.sin(angles)[:, None, :])


def rotate(head_view, cosine, sine):
    half_rot = ROT // 2
    turned = head_view[..., :ROT]
    swapped = jnp.concatenate([-turned[..., half_rot:], turned[..., :half_rot]], -1)
    return jnp.concatenate([turned * cosine + swapped * sine, head_view[..., ROT:]], -1)


def norm_apply(tokens, scale_gain, shift_bias):
    centred = tokens - jnp.mean(tokens, 1, keepdims=True)
    rstd = lax.rsqrt(jnp.mean(centred * centred, 1, keepdims=True) + NORM_EPS)
    return centred * rstd * scale_gain + shift_bias


def contract_last(left, right):
    return lax.dot_general(
        left, right, (((1,), (1,)), ((), ())), preferred_element_type=jnp.float32
    )


def visible_mask(query_places, key_places, limits):
    reach = jnp.maximum(query_places[None, :], limits[:, None] - 1)
    return (key_places[None, None, :] <= reach[:, :, None])[:, None]


def forward_part(tokens, limits, params, first_place, cosine, sine):
    (
        qkv_weight,
        dense_weight,
        fc1_weight,
        fc2_weight,
        norm_gain,
        norm_shift,
        qkv_bias,
        dense_bias,
        fc1_bias,
        fc2_bias,
    ) = params
    seq_count, local_len, model_width = tokens.shape
    score_scale = 1.0 / math.sqrt(HEAD)
    flat_rows = tokens.reshape(seq_count * local_len, model_width).astype(jnp.float32)
    normed_low = norm_apply(
        flat_rows, norm_gain.astype(jnp.float32), norm_shift.astype(jnp.float32)
    ).astype(jnp.bfloat16)
    merged = contract_last(normed_low, qkv_weight) + qkv_bias.astype(jnp.float32)
    head_view = merged.reshape(seq_count, local_len, 3, HEADS, HEAD)
    query_low = rotate(head_view[:, :, 0], cosine, sine).astype(jnp.bfloat16)
    key_low = (
        rotate(head_view[:, :, 1], cosine, sine)
        .astype(jnp.bfloat16)
        .reshape(seq_count, local_len, model_width)
    )
    value_low = head_view[:, :, 2].astype(jnp.bfloat16).reshape(seq_count, local_len, model_width)
    query_places = first_place + jnp.arange(local_len, dtype=jnp.int32)
    row_top = jnp.full((seq_count, HEADS, local_len), MASKED_LOW, jnp.float32)
    keys_piece = lax.all_gather(key_low, "seq", axis=1, tiled=True)
    values_piece = lax.all_gather(value_low, "seq", axis=1, tiled=True)
    piece_len = keys_piece.shape[1]
    keys_piece = keys_piece.reshape(seq_count, piece_len, HEADS, HEAD)
    values_piece = values_piece.reshape(seq_count, piece_len, HEADS, HEAD)
    scores = (
        jnp.einsum("sqhd,skhd->shqk", query_low, keys_piece, preferred_element_type=jnp.float32)
        * score_scale
    )
    visible = visible_mask(query_places, jnp.arange(piece_len, dtype=jnp.int32), limits)
    masked = jnp.where(visible, scores, MASKED_LOW)
    new_top = jnp.maximum(row_top, jnp.max(masked, -1))
    exp_weights = jnp.where(visible, jnp.exp(masked - new_top[..., None]), 0.0)
    row_total = jnp.sum(exp_weights, -1)
    accum = jnp.einsum(
        "shqk,skhd->shqd",
        exp_weights.astype(jnp.bfloat16),
        values_piece,
        preferred_element_type=jnp.float32,
    )
    row_top, row_total, accum = (new_top, row_total, accum)
    mixed = accum / row_total[..., None]
    log_total = row_top + jnp.log(row_total)
    mixed_low = (
        mixed.transpose(0, 2, 1, 3).reshape(seq_count * local_len, model_width).astype(jnp.bfloat16)
    )
    hidden_pre = contract_last(normed_low, fc1_weight) + fc1_bias.astype(jnp.float32)
    act_low = gelu_tanh(hidden_pre).astype(jnp.bfloat16)
    result = (
        flat_rows
        + jnp.dot(mixed_low, dense_weight, preferred_element_type=jnp.float32)
        + dense_bias.astype(jnp.float32)
    )
    result = (
        result
        + jnp.dot(act_low, fc2_weight, preferred_element_type=jnp.float32)
        + fc2_bias.astype(jnp.float32)
    )
    saved_parts = (
        flat_rows,
        normed_low,
        query_low,
        key_low,
        value_low,
        mixed,
        log_total,
        hidden_pre,
        act_low,
        mixed_low,
    )
    return (result.astype(jnp.bfloat16).reshape(tokens.shape), saved_parts)


def backward_part(grad_low, limits, params, first_place, cosine, sine, saved_parts):
    (
        qkv_weight,
        dense_weight,
        fc1_weight,
        fc2_weight,
        norm_gain,
        norm_shift,
        qkv_bias,
        dense_bias,
        fc1_bias,
        fc2_bias,
    ) = params
    (
        flat_rows,
        normed_low,
        query_low,
        key_low,
        value_low,
        mixed,
        log_total,
        hidden_pre,
        act_low,
        mixed_low,
    ) = saved_parts
    seq_count, local_len, model_width = grad_low.shape
    score_scale = 1.0 / math.sqrt(HEAD)
    grad_rows_low = grad_low.reshape(seq_count * local_len, model_width)
    grad_rows = grad_rows_low.astype(jnp.float32)
    grad_mixed_low = contract_last(grad_rows_low, dense_weight).astype(jnp.bfloat16)
    grad_act = contract_last(grad_rows_low, fc2_weight)
    gelu_pull = jax.vjp(gelu_tanh, hidden_pre)[1]
    grad_hidden_low = gelu_pull(grad_act)[0].astype(jnp.bfloat16)
    grad_out_heads = grad_mixed_low.reshape(seq_count, local_len, HEADS, HEAD)
    delta = jnp.sum(grad_out_heads.astype(jnp.float32).transpose(0, 2, 1, 3) * mixed, -1)
    stats_lse, stats_delta = (
        lax.all_gather(log_total.transpose(0, 2, 1), "seq", axis=1, tiled=True),
        lax.all_gather(delta.transpose(0, 2, 1), "seq", axis=1, tiled=True),
    )
    local_places = first_place + jnp.arange(local_len, dtype=jnp.int32)
    key_heads = key_low.reshape(seq_count, local_len, HEADS, HEAD)
    value_heads = value_low.reshape(seq_count, local_len, HEADS, HEAD)
    keys_piece = lax.all_gather(key_low, "seq", axis=1, tiled=True)
    values_piece = lax.all_gather(value_low, "seq", axis=1, tiled=True)
    piece_len = keys_piece.shape[1]
    keys_piece = keys_piece.reshape(seq_count, piece_len, HEADS, HEAD)
    values_piece = values_piece.reshape(seq_count, piece_len, HEADS, HEAD)
    scores = (
        jnp.einsum("sqhd,skhd->shqk", query_low, keys_piece, preferred_element_type=jnp.float32)
        * score_scale
    )
    visible = visible_mask(local_places, jnp.arange(piece_len, dtype=jnp.int32), limits)
    prob_rows = jnp.where(visible, jnp.exp(scores - log_total[..., None]), 0.0)
    grad_probs = jnp.einsum(
        "sqhd,skhd->shqk", grad_out_heads, values_piece, preferred_element_type=jnp.float32
    )
    grad_scores = (prob_rows * (grad_probs - delta[..., None])).astype(jnp.bfloat16)
    grad_query = score_scale * jnp.einsum(
        "shqk,skhd->sqhd", grad_scores, keys_piece, preferred_element_type=jnp.float32
    )
    query_flat = query_low.reshape(seq_count, local_len, model_width)
    grad_out_flat = grad_mixed_low.reshape(seq_count, local_len, model_width)
    queries_piece = lax.all_gather(query_flat, "seq", axis=1, tiled=True)
    grad_out_piece = lax.all_gather(grad_out_flat, "seq", axis=1, tiled=True)
    piece_len = queries_piece.shape[1]
    queries_piece = queries_piece.reshape(seq_count, piece_len, HEADS, HEAD)
    grad_out_piece = grad_out_piece.reshape(seq_count, piece_len, HEADS, HEAD)
    piece_lse = stats_lse.transpose(0, 2, 1)
    piece_delta = stats_delta.transpose(0, 2, 1)
    scores = (
        jnp.einsum("sqhd,skhd->shqk", queries_piece, key_heads, preferred_element_type=jnp.float32)
        * score_scale
    )
    visible = visible_mask(jnp.arange(piece_len, dtype=jnp.int32), local_places, limits)
    prob_rows = jnp.where(visible, jnp.exp(scores - piece_lse[..., None]), 0.0)
    grad_probs = jnp.einsum(
        "sqhd,skhd->shqk", grad_out_piece, value_heads, preferred_element_type=jnp.float32
    )
    grad_scores = (prob_rows * (grad_probs - piece_delta[..., None])).astype(jnp.bfloat16)
    grad_values = jnp.einsum(
        "shqk,sqhd->skhd",
        prob_rows.astype(jnp.bfloat16),
        grad_out_piece,
        preferred_element_type=jnp.float32,
    )
    grad_keys = score_scale * jnp.einsum(
        "shqk,sqhd->skhd", grad_scores, queries_piece, preferred_element_type=jnp.float32
    )
    grad_keys, grad_values = (grad_keys, grad_values)
    paired = jnp.stack([grad_query, grad_keys], 0)
    rotate_pull = jax.vjp(partial(rotate, cosine=cosine, sine=sine), paired)[1]
    unturned = rotate_pull(paired)[0]
    grad_merged_low = (
        jnp.stack([unturned[0], unturned[1], grad_values], 2)
        .reshape(seq_count * local_len, 3 * model_width)
        .astype(jnp.bfloat16)
    )
    grad_normed = jnp.dot(
        grad_merged_low, qkv_weight, preferred_element_type=jnp.float32
    ) + jnp.dot(grad_hidden_low, fc1_weight, preferred_element_type=jnp.float32)
    norm_pull = jax.vjp(
        norm_apply, flat_rows, norm_gain.astype(jnp.float32), norm_shift.astype(jnp.float32)
    )[1]
    grad_flat, grad_gain, grad_shift = norm_pull(grad_normed)
    input_grad = (grad_rows + grad_flat).reshape(seq_count, local_len, model_width)
    bias_sums = jnp.sum(grad_rows, 0)
    small_terms = (
        grad_gain,
        grad_shift,
        jnp.sum(grad_merged_low.astype(jnp.float32), 0),
        bias_sums,
        jnp.sum(grad_hidden_low.astype(jnp.float32), 0),
        bias_sums,
    )
    operand_set = (normed_low, grad_merged_low, mixed_low, grad_rows_low, grad_hidden_low, act_low)
    return (input_grad, small_terms, operand_set)


def terms_builder(operand_set, row_sizes, model_width, row_count):
    normed_all, grad_merged_all, mixed_all, grad_out_all, grad_hidden_all, act_all = operand_set
    rows_qkv, rows_dense, rows_fc1, rows_fc2 = row_sizes
    block_rows = rows_qkv + rows_dense + rows_fc1 + rows_fc2
    block_count = row_count // block_rows

    def outer_term(left, right, block_width):
        term = lax.dot_general(
            left, right, (((0,), (0,)), ((), ())), preferred_element_type=jnp.float32
        )
        return term.reshape(block_count, block_width, model_width)

    term_parts = [
        outer_term(grad_merged_all, normed_all, rows_qkv),
        outer_term(mixed_all, grad_out_all, rows_dense),
        outer_term(grad_hidden_all, normed_all, rows_fc1),
        outer_term(act_all, grad_out_all, rows_fc2),
    ]
    return jnp.concatenate(term_parts, 1).reshape(row_count, model_width)


def on_device(
    hidden_in,
    cotangent,
    prefix_len,
    qkv_weight,
    dense_weight,
    fc1_weight,
    fc2_weight,
    norm_gain,
    norm_shift,
    qkv_bias,
    dense_bias,
    fc1_bias,
    fc2_bias,
):
    micro_count, seq_count, local_len, model_width = hidden_in.shape
    first_place = lax.axis_index("seq") * local_len
    cosine, sine = rotary_tables(first_place, local_len)
    row_sizes = (
        qkv_weight.shape[0],
        dense_weight.shape[0],
        fc1_weight.shape[0],
        fc2_weight.shape[0],
    )
    block_rows = row_sizes[0] + row_sizes[1] + row_sizes[2] + row_sizes[3]
    params = (
        lax.all_gather(qkv_weight, ("dp", "seq"), axis=0, tiled=True),
        lax.all_gather(dense_weight, ("dp", "seq"), axis=0, tiled=True),
        lax.all_gather(fc1_weight, ("dp", "seq"), axis=0, tiled=True),
        lax.all_gather(fc2_weight, ("dp", "seq"), axis=0, tiled=True),
        lax.all_gather(norm_gain, ("dp", "seq"), axis=0, tiled=True),
        lax.all_gather(norm_shift, ("dp", "seq"), axis=0, tiled=True),
        lax.all_gather(qkv_bias, ("dp", "seq"), axis=0, tiled=True),
        lax.all_gather(dense_bias, ("dp", "seq"), axis=0, tiled=True),
        lax.all_gather(fc1_bias, ("dp", "seq"), axis=0, tiled=True),
        lax.all_gather(fc2_bias, ("dp", "seq"), axis=0, tiled=True),
    )
    outputs = []
    input_grads = []
    small_totals = None
    operand_lists = []
    weight_rows = None
    for batch_index in range(micro_count):
        limits = prefix_len[batch_index]
        result, saved_parts = forward_part(
            hidden_in[batch_index], limits, params, first_place, cosine, sine
        )
        input_grad, small_terms, operand_set = backward_part(
            cotangent[batch_index], limits, params, first_place, cosine, sine, saved_parts
        )
        outputs.append(result)
        input_grads.append(input_grad)
        operand_lists.append(operand_set)
        if small_totals is None:
            small_totals = small_terms
        else:
            small_totals = tuple(
                (old_sum + new_term for old_sum, new_term in zip(small_totals, small_terms))
            )
    joined_set = tuple(
        (jnp.concatenate([entry[place] for entry in operand_lists], 0) for place in range(6))
    )
    weight_rows = lax.psum_scatter(
        terms_builder(
            joined_set, row_sizes, model_width, block_rows * lax.axis_size(("dp", "seq"))
        ),
        ("dp", "seq"),
        scatter_dimension=0,
        tiled=True,
    )
    rows_qkv, rows_dense, rows_fc1, rows_fc2 = row_sizes
    qkv_grad = weight_rows[:rows_qkv]
    dense_grad = weight_rows[rows_qkv : rows_qkv + rows_dense]
    fc1_grad = weight_rows[rows_qkv + rows_dense : rows_qkv + rows_dense + rows_fc1]
    fc2_grad = weight_rows[rows_qkv + rows_dense + rows_fc1 :]
    gain_grad, shift_grad, qkv_bias_grad, dense_bias_grad, fc1_bias_grad, fc2_bias_grad = (
        lax.psum_scatter(small_totals[0], ("dp", "seq"), scatter_dimension=0, tiled=True),
        lax.psum_scatter(small_totals[1], ("dp", "seq"), scatter_dimension=0, tiled=True),
        lax.psum_scatter(small_totals[2], ("dp", "seq"), scatter_dimension=0, tiled=True),
        lax.psum_scatter(small_totals[3], ("dp", "seq"), scatter_dimension=0, tiled=True),
        lax.psum_scatter(small_totals[4], ("dp", "seq"), scatter_dimension=0, tiled=True),
        lax.psum_scatter(small_totals[5], ("dp", "seq"), scatter_dimension=0, tiled=True),
    )
    return (
        jnp.stack(outputs, 0),
        jnp.stack(input_grads, 0),
        qkv_grad,
        dense_grad,
        fc1_grad,
        fc2_grad,
        gain_grad,
        shift_grad,
        qkv_bias_grad,
        dense_bias_grad,
        fc1_bias_grad,
        fc2_bias_grad,
    )


MESH = pl.DeviceIdType.MESH
BF = jnp.bfloat16
F32 = jnp.float32


def place():
    d = lax.axis_index("dp")
    s = lax.axis_index("seq")
    return d, s, s // 4, (s // 2) % 2, s % 2


def seq_of(z, y, c):
    return z * 4 + y * 2 + c


def send(src, dst, ssem, rsem, target):
    pltpu.make_async_remote_copy(
        src_ref=src, dst_ref=dst, send_sem=ssem, recv_sem=rsem, device_id=target, device_id_type=MESH
    ).start()


def local(src, dst, sem):
    pltpu.make_async_copy(src, dst, sem).start()


def await_bytes(ref, sem):
    pltpu.make_async_copy(ref, ref, sem).wait()


def signal(sem, target):
    pl.semaphore_signal(sem, inc=1, device_id=target, device_id_type=MESH)


class Gather:
    SEMS = 38

    def __init__(self, src, G, sem, cut):
        self.src, self.G, self.sem, self.cut, self.width = src, G, sem, cut, G.shape[-1]

    def first(self, zz, yy):
        d, s, z, y, c = place()
        return self.G.at[zz, yy, c, :, slice(0, self.cut)]

    def pair(self, zz):
        d, s, z, y, c = place()
        return self.G.at[zz, :, c, :, slice(self.cut, self.width)]

    def along_z(self, src, dst, up, down, recv, to_up, to_down):
        d, s, z, y, c = place()
        if to_up:

            @pl.when(z < 3)
            def _():
                send(src, dst, self.sem.at[up], self.sem.at[recv], (d, s + 4))

        if to_down:

            @pl.when(z > 0)
            def _():
                send(src, dst, self.sem.at[down], self.sem.at[recv], (d, s - 4))

    def start_rest(self):
        d, s, z, y, c = place()
        rest = slice(self.cut, self.width)
        over = (d, seq_of(z, 1 - y, c))
        send(self.src.at[:, rest], self.G.at[z, y, c, :, rest], self.sem.at[32], self.sem.at[33], over)

    def start_first(self):
        d, s, z, y, c = place()
        src = self.src.at[:, slice(0, self.cut)]
        self.along_z(src, self.first(z, y), 4 + z, 0 + z, 8 + z, True, True)
        over = (d, seq_of(z, 1 - y, c))
        send(src, self.first(z, y), self.sem.at[24 + z], self.sem.at[28 + z], over)

    def pairs(self):
        d, s, z, y, c = place()
        await_bytes(self.G.at[z, 1 - y, c, :, slice(self.cut, self.width)], self.sem.at[33])
        self.along_z(self.pair(z), self.pair(z), 16 + z, 12 + z, 20 + z, True, True)

    def hop(self, h):
        d, s, z, y, c = place()
        for below in (True, False):
            zz = z - h if below else z + h

            @pl.when(z >= h if below else z + h <= 3)
            def _():
                chunk = self.first(zz, y)
                await_bytes(chunk, self.sem.at[8 + zz])
                self.along_z(chunk, chunk, 4 + zz, 0 + zz, 8 + zz, below, not below)
                send(chunk, chunk, self.sem.at[24 + zz], self.sem.at[28 + zz], (d, seq_of(z, 1 - y, c)))

    def pair_hop(self, h):
        d, s, z, y, c = place()
        for below in (True, False):
            zz = z - h if below else z + h

            @pl.when(z >= h if below else z + h <= 3)
            def _():
                chunk = self.pair(zz)
                await_bytes(chunk, self.sem.at[20 + zz])
                self.along_z(chunk, chunk, 16 + zz, 12 + zz, 20 + zz, below, not below)

    def own_line(self):
        d, s, z, y, c = place()
        line = self.G.at[:, y, c]
        send(line, line, self.sem.at[34], self.sem.at[36], (d, seq_of(z, y, 1 - c)))

    def other_line(self):
        d, s, z, y, c = place()
        for zz in range(4):
            await_bytes(self.first(zz, 1 - y), self.sem.at[28 + zz])
        line = self.G.at[:, 1 - y, c]
        send(line, line, self.sem.at[35], self.sem.at[37], (d, seq_of(z, y, 1 - c)))

    def arrived(self):
        for k in range(2):
            await_bytes(self.G.at[:, 0, 0], self.sem.at[36 + k])

    def drain(self):
        d, s, z, y, c = place()
        await_bytes(self.pair(0).at[0], self.sem.at[32])
        for zz in range(4):
            await_bytes(self.first(0, 0), self.sem.at[24 + zz])

            @pl.when((z < 3) & (zz <= z))
            def _():
                await_bytes(self.first(0, 0), self.sem.at[4 + zz])
                await_bytes(self.pair(0), self.sem.at[16 + zz])

            @pl.when((z > 0) & (zz >= z))
            def _():
                await_bytes(self.first(0, 0), self.sem.at[0 + zz])
                await_bytes(self.pair(0), self.sem.at[12 + zz])

        for k in range(2):
            await_bytes(self.G.at[:, 0, 0], self.sem.at[34 + k])


class Scatter:
    SEMS = 32

    def __init__(self, P, RC, RY, ZA, ZB, YB, TOT, sem, free, reuse, cut):
        self.P, self.RC, self.RY, self.ZA, self.ZB, self.YB, self.TOT = P, RC, RY, ZA, ZB, YB, TOT
        self.sem, self.free, self.reuse, self.cut = sem, free, reuse, cut
        self.head, self.rest = slice(0, cut), slice(cut, P.shape[-1])

    def start(self):
        d, s, z, y, c = place()
        if self.reuse:
            pl.semaphore_wait(self.free.at[0], 1)
        for k, row in ((0, 1 - y), (1, y)):
            send(
                self.P.at[:, row, 1 - c], self.RC.at[:, row], self.sem.at[k], self.sem.at[2 + k], (d, seq_of(z, y, 1 - c))
            )

    def cores(self):
        d, s, z, y, c = place()
        await_bytes(self.RC.at[:, 0], self.sem.at[2])
        await_bytes(self.RC.at[:, 0], self.sem.at[3])
        if self.reuse:
            pl.semaphore_wait(self.free.at[1], 1)

            @pl.when(z < 3)
            def _():
                pl.semaphore_wait(self.free.at[2], 1)

            @pl.when(z > 0)
            def _():
                pl.semaphore_wait(self.free.at[3], 1)

    def targets(self, h, act):
        d, s, z, y, c = place()
        for below in (True, False):
            zz = z - h if below else z + h

            @pl.when(z >= h if below else z + h <= 3)
            def _():
                act(below, zz)

    def over_y(self, h):
        d, s, z, y, c = place()

        def one(below, zz):
            chunk = self.P.at[zz, 1 - y, c, :, self.head]
            chunk[...] = (chunk[...].astype(F32) + self.RC[zz, 1 - y, :, self.head].astype(F32)).astype(BF)
            send(chunk, self.RY.at[zz], self.sem.at[4 + zz], self.sem.at[8 + zz], (d, seq_of(z, 1 - y, c)))

        if h == 0:
            one(True, z)
        else:
            self.targets(h, one)

    def add_beyond(self, chunk, Z, sems, below, zz):
        d, s, z, y, c = place()

        @pl.when(z < 3 if below else z > 0)
        def _():
            await_bytes(Z.at[zz], self.sem.at[sems + zz])
            chunk[...] = (chunk[...].astype(F32) + Z[zz].astype(F32)).astype(BF)

    def pass_on(self, chunk, Z, ssem, sems, below, zz, h):
        d, s, z, y, c = place()
        slot = 4 if h == 1 and not below else zz
        target = (d, s - 4) if below else (d, s + 4)
        send(chunk, Z.at[slot], self.sem.at[ssem + zz], self.sem.at[sems + slot], target)

    def along_z(self, h):
        d, s, z, y, c = place()

        def one(below, zz):
            await_bytes(self.RY.at[zz], self.sem.at[8 + zz])
            chunk = self.P.at[zz, y, c, :, self.head]
            chunk[...] = (
                chunk[...].astype(F32) + self.RC[zz, y, :, self.head].astype(F32) + self.RY[zz].astype(F32)
            ).astype(BF)
            self.add_beyond(chunk, self.ZA, 16, below, zz)
            self.pass_on(chunk, self.ZA, 12, 16, below, zz, h)

        self.targets(h, one)

    def pairs_along_z(self, h):
        d, s, z, y, c = place()

        def one(below, zz):
            chunk = self.P.at[zz, :, c, :, self.rest]
            chunk[...] = (chunk[...].astype(F32) + self.RC[zz, :, :, self.rest].astype(F32)).astype(BF)
            self.add_beyond(chunk, self.ZB, 25, below, zz)
            self.pass_on(chunk, self.ZB, 21, 25, below, zz, h)

        self.targets(h, one)

    def pairs_over_y(self):
        d, s, z, y, c = place()
        chunk = self.P.at[z, :, c, :, self.rest]
        chunk[...] = (chunk[...].astype(F32) + self.RC[z, :, :, self.rest].astype(F32)).astype(BF)

        @pl.when(z < 3)
        def _():
            await_bytes(self.ZB.at[z], self.sem.at[25 + z])
            chunk[...] = (chunk[...].astype(F32) + self.ZB[z].astype(F32)).astype(BF)

        @pl.when(z > 0)
        def _():
            await_bytes(self.ZB.at[4], self.sem.at[29])
            chunk[...] = (chunk[...].astype(F32) + self.ZB[4].astype(F32)).astype(BF)

        other = self.P.at[z, 1 - y, c, :, self.rest]
        send(other, self.YB, self.sem.at[30], self.sem.at[31], (d, seq_of(z, 1 - y, c)))

    def total(self):
        d, s, z, y, c = place()
        await_bytes(self.RY.at[z], self.sem.at[8 + z])
        head, rest = self.head, self.rest
        self.TOT[:, head] = (
            self.P[z, y, c, :, head].astype(F32) + self.RC[z, y, :, head].astype(F32) + self.RY[z].astype(F32)
        )

        @pl.when(z < 3)
        def _():
            await_bytes(self.ZA.at[z], self.sem.at[16 + z])
            self.TOT[:, head] += self.ZA[z].astype(F32)

        @pl.when(z > 0)
        def _():
            await_bytes(self.ZA.at[4], self.sem.at[20])
            self.TOT[:, head] += self.ZA[4].astype(F32)

        await_bytes(self.YB, self.sem.at[31])
        self.TOT[:, rest] = self.P[z, y, c, :, rest].astype(F32) + self.YB[...].astype(F32)
        return self.TOT[...]

    def release(self):
        d, s, z, y, c = place()
        signal(self.free.at[0], (d, seq_of(z, y, 1 - c)))
        signal(self.free.at[1], (d, seq_of(z, 1 - y, c)))

        @pl.when(z < 3)
        def _():
            signal(self.free.at[3], (d, s + 4))

        @pl.when(z > 0)
        def _():
            signal(self.free.at[2], (d, s - 4))

    def drain(self):
        d, s, z, y, c = place()
        for k in range(2):
            await_bytes(self.RC.at[:, 0], self.sem.at[k])
        for zz in range(4):
            await_bytes(self.RY.at[0], self.sem.at[4 + zz])

            @pl.when(z != zz)
            def _():
                await_bytes(self.ZA.at[0], self.sem.at[12 + zz])
                await_bytes(self.ZB.at[0], self.sem.at[21 + zz])

        await_bytes(self.YB, self.sem.at[30])


def everyone(act):
    d, s, z, y, c = place()

    def one(k, carry):
        other = lax.rem(d * 16 + s + k, 32)
        act((other // 16, other % 16), other)
        return carry

    lax.fori_loop(1, 32, one, 0)


def greet_all():
    barrier = pltpu.get_barrier_semaphore()
    everyone(lambda device, slot: signal(barrier, device))
    pl.semaphore_wait(barrier, 31)


class Exchange:
    def __init__(self, src, dst, ss, rs, same):
        self.src, self.dst, self.ss, self.rs, self.same = src, dst, ss, rs, same

    def start(self):
        d, s, z, y, c = place()
        me = d * 16 + s

        def one(device, slot):
            src = self.src if self.same else self.src.at[slot]
            send(src, self.dst.at[me], self.ss.at[0], self.rs.at[0], device)

        everyone(one)

    def arrived(self):
        await_bytes(self.dst.at[pl.ds(0, 31)], self.rs.at[0])

    def drain(self):
        await_bytes(self.dst.at[pl.ds(0, 31)], self.ss.at[0])


QB = 256


def dot_nt(left, right):
    return lax.dot_general(left, right, (((1,), (1,)), ((), ())), preferred_element_type=F32)


def dot_nn(left, right):
    return jnp.dot(left, right, preferred_element_type=F32)


def head_lanes(shape, dim):
    return lax.broadcasted_iota(jnp.int32, shape, dim) // HEAD


def swap_halves(rows):
    lane = lax.broadcasted_iota(jnp.int32, rows.shape, 1) % HEAD
    return jnp.where(lane < ROT // 2, pltpu.roll(rows, 128 - ROT // 2, 1), pltpu.roll(rows, ROT // 2, 1))


def front_tile(R, m, zt):
    width = R.N.shape[-1]
    n = R.N[m, zt].reshape(QB, width)
    rows = pl.ds(pl.multiple_of(zt * QB, QB), QB)
    merged = dot_nt(n, R.Wq[...].reshape(384, width)) + R.bq[...]
    cos, sin = R.cos[rows, :], R.sin[rows, :]
    query, key, value = merged[:, :128], merged[:, 128:256], merged[:, 256:]
    query = (query * cos + swap_halves(query) * sin).astype(BF)
    key = (key * cos + swap_halves(key) * sin).astype(BF)
    value = value.astype(BF)
    R.Q[rows, :] = query * jnp.asarray(0.125, BF)
    R.K[rows, :] = key
    R.V[rows, :] = value
    R.KT[zt] = key.T
    R.VT[zt] = value.T
    gm = dot_nt(R.DY[m, zt].reshape(QB, width), R.Wd[...].reshape(128, width)).astype(BF)
    R.GM[rows, :] = gm


def hidden_tile(R, m, zt):
    width = R.N.shape[-1]
    rows = pl.ds(pl.multiple_of(zt * QB, QB), QB)
    pre = dot_nt(R.N[m, zt].reshape(QB, width), R.W1[...].reshape(512, width)) + R.b1[...]
    grad = dot_nt(R.DY[m, zt].reshape(QB, width), R.W2[...].reshape(512, width))
    square = pre * pre
    turn = jnp.tanh(TANH_FACTOR * (pre + CUBIC_FACTOR * square * pre))
    half = 0.5 + 0.5 * turn
    slope = half + (0.5 * TANH_FACTOR) * pre * (1.0 - turn * turn) * (1.0 + 3.0 * CUBIC_FACTOR * square)
    R.ACT[m, rows, :] = (pre * half).astype(BF)
    gh = (slope * grad).astype(BF)
    R.GH[m, rows, :] = gh
    R.gh_sum[...] += jnp.sum(gh.astype(F32), 0, keepdims=True)


def attention_tile(R, m, qb, limit):
    (attention_wide if qb < 3 else attention_tall)(R, m, qb, limit)


def attention_wide(R, m, qb, limit):
    chunks = max(2, qb + 1)
    ext = chunks * QB
    q_rows = slice(qb * QB, (qb + 1) * QB)
    zero = jnp.asarray(0, BF)
    lane_head = head_lanes((QB, 128), 1)
    q0, gm0 = R.Q[q_rows, :], R.GM[q_rows, :]
    q = jnp.concatenate([jnp.where(lane_head == h, q0, zero) for h in range(2)], 0)
    gm = jnp.concatenate([jnp.where(lane_head == h, gm0, zero) for h in range(2)], 0)
    reach = jnp.maximum(qb * QB + lax.broadcasted_iota(jnp.int32, (1, 2 * QB), 1) % QB, limit - 1)
    s = dot_nt(R.K[:ext, :], q)
    parts = []
    for kc in range(chunks):
        part = s[kc * QB : (kc + 1) * QB]
        if kc >= qb:
            place_j = kc * QB + lax.broadcasted_iota(jnp.int32, (QB, 2 * QB), 0)
            part = jnp.where(place_j <= reach, part, MASKED_LOW)
        parts.append(part)
    s = jnp.concatenate(parts, 0)
    top = jnp.max(s, 0, keepdims=True)
    e = jnp.exp(s - top)
    total = jnp.sum(e, 0, keepdims=True)
    inverse = 1.0 / total
    eb = e.astype(BF)
    mix = None
    for kc in range(chunks):
        term = dot_nn(R.VT[kc], eb[kc * QB : (kc + 1) * QB])
        mix = term if mix is None else mix + term
    mix = mix * inverse
    row_head = head_lanes((128, 2 * QB), 0)
    lane_block = lax.broadcasted_iota(jnp.int32, (128, 2 * QB), 1) // QB
    own = row_head == lane_block
    gm_t = gm0.astype(F32).T
    gm_t = jnp.concatenate([gm_t, gm_t], 1)
    delta = jnp.sum(jnp.where(own, gm_t * mix, 0.0), 0, keepdims=True)
    p = e * inverse
    gp = dot_nt(R.V[:ext, :], gm)
    ds = (p * (gp - delta)).astype(BF)
    dq = None
    for kc in range(chunks):
        term = dot_nn(R.KT[kc], ds[kc * QB : (kc + 1) * QB])
        dq = term if dq is None else dq + term
    dk = dot_nn(ds, q)
    dv = dot_nn(p.astype(BF), gm)
    done = 0 if qb == 0 else max(2, qb) * QB
    if done:
        R.DK[:done, :] += dk[:done]
        R.DV[:done, :] += dv[:done]
    if done < ext:
        R.DK[done:ext, :] = dk[done:]
        R.DV[done:ext, :] = dv[done:]
    mixed_t = jnp.where(row_head[:, :QB] == 0, mix[:, :QB], mix[:, QB:])
    dq_t = jnp.where(row_head[:, :QB] == 0, dq[:, :QB], dq[:, QB:])
    R.MM[m, q_rows, 384:] = mixed_t.T.astype(BF)
    grad_query = dq_t.T * 0.125
    cos, sin = R.cos[q_rows, :], R.sin[q_rows, :]
    grad_query = (grad_query * cos - swap_halves(grad_query) * sin).astype(BF)
    R.MM[m, q_rows, :128] = grad_query
    R.mm_sum[:, :128] += jnp.sum(grad_query.astype(F32), 0, keepdims=True)


def attention_tall(R, m, qb, limit):
    chunks = max(2, qb + 1)
    ext = chunks * QB
    q_rows = slice(qb * QB, (qb + 1) * QB)
    zero = jnp.asarray(0, BF)
    lane_head = head_lanes((QB, 128), 1)
    row_head = head_lanes((128, QB), 0)
    reach = jnp.maximum(qb * QB + lax.broadcasted_iota(jnp.int32, (1, QB), 1), limit - 1)
    mixed_t, dq_t = [], []
    done = max(2, qb) * QB
    gm_t = R.GM[q_rows, :].astype(F32).T
    for h in range(2):
        q = jnp.where(lane_head == h, R.Q[q_rows, :], zero)
        gm = jnp.where(lane_head == h, R.GM[q_rows, :], zero)
        s = dot_nt(R.K[:ext, :], q)
        parts = []
        for kc in range(chunks):
            part = s[kc * QB : (kc + 1) * QB]
            if kc >= qb:
                place_j = kc * QB + lax.broadcasted_iota(jnp.int32, (QB, QB), 0)
                part = jnp.where(place_j <= reach, part, MASKED_LOW)
            parts.append(part)
        s = jnp.concatenate(parts, 0)
        gp = dot_nt(R.V[:ext, :], gm)
        top = jnp.max(s, 0, keepdims=True)
        e = jnp.exp(s - top)
        total = jnp.sum(e, 0, keepdims=True)
        inverse = 1.0 / total
        eb = e.astype(BF)
        mix = None
        for kc in range(chunks):
            term = dot_nn(R.VT[kc], eb[kc * QB : (kc + 1) * QB])
            mix = term if mix is None else mix + term
        mix = mix * inverse
        delta = jnp.sum(jnp.where(row_head == h, gm_t * mix, 0.0), 0, keepdims=True)
        p = e * inverse
        ds = (p * (gp - delta)).astype(BF)
        dq = None
        for kc in range(chunks):
            term = dot_nn(R.KT[kc], ds[kc * QB : (kc + 1) * QB])
            dq = term if dq is None else dq + term
        dk, dv = dot_nn(ds, q), dot_nn(p.astype(BF), gm)
        fresh = 0 if h else ext - done
        R.DK[: ext - fresh, :] += dk[: ext - fresh]
        R.DV[: ext - fresh, :] += dv[: ext - fresh]
        if fresh:
            R.DK[done:ext, :] = dk[done:]
            R.DV[done:ext, :] = dv[done:]
        mixed_t.append(mix)
        dq_t.append(dq)
    R.MM[m, q_rows, 384:] = jnp.where(row_head == 0, mixed_t[0], mixed_t[1]).T.astype(BF)
    grad_query = jnp.where(row_head == 0, dq_t[0], dq_t[1]).T * 0.125
    cos, sin = R.cos[q_rows, :], R.sin[q_rows, :]
    grad_query = (grad_query * cos - swap_halves(grad_query) * sin).astype(BF)
    R.MM[m, q_rows, :128] = grad_query
    R.mm_sum[:, :128] += jnp.sum(grad_query.astype(F32), 0, keepdims=True)


def key_tile(R, m, i):
    rows = pl.ds(pl.multiple_of(i * QB, QB), QB)
    grad_key = R.DK[rows, :]
    cos, sin = R.cos[rows, :], R.sin[rows, :]
    grad_key = (grad_key * cos - swap_halves(grad_key) * sin).astype(BF)
    grad_value = R.DV[rows, :].astype(BF)
    R.MM[m, rows, 128:256] = grad_key
    R.MM[m, rows, 256:384] = grad_value
    R.mm_sum[:, 128:256] += jnp.sum(grad_key.astype(F32), 0, keepdims=True)
    R.mm_sum[:, 256:384] += jnp.sum(grad_value.astype(F32), 0, keepdims=True)


def out_tile(R, m, i, P):
    rows = pl.ds(pl.multiple_of(i * QB, QB), QB)
    width = R.N.shape[-1]
    mixed = R.MM[m, rows, 384:]
    act = R.ACT[m, rows, :]
    for col in range(0, width, 512):
        cols = slice(col, col + 512)
        total = dot_nn(mixed, R.Wd[:, :, cols].reshape(128, 512)) + dot_nn(act, R.W2[:, :, cols].reshape(512, 512))
        P[i, :, :, :, cols] = total.astype(BF).reshape(2, 2, 64, 512)


def grad_tile(R, m, i, P):
    rows = pl.ds(pl.multiple_of(i * QB, QB), QB)
    width = R.N.shape[-1]
    merged = R.MM[m, rows, :384]
    gh = R.GH[m, rows, :]
    for col in range(0, width, 512):
        cols = slice(col, col + 512)
        total = dot_nn(merged, R.Wq[:, :, cols].reshape(384, 512)) + dot_nn(gh, R.W1[:, :, cols].reshape(512, 512))
        P[i, :, :, :, cols] = total.astype(BF).reshape(2, 2, 64, 512)


def turn_tile(R, src, m, i):
    place_i = (m * 4 + i) * QB
    R.AT[:, place_i : place_i + QB] = src[m, i * QB : (i + 1) * QB, :].T


D0, D1, N0, N1, G0, G1, O0, O1 = range(8)
REST, FIRST, PAIRS, OWN, OTHER, HOP, PAIR_HOP, CORES, OVER_Y, ALONG_Z, PAIRS_Z, PAIRS_Y, TOTAL = range(13)
QKV, OWNERS = (-1, 0, 0), (-2, 0, 0)
(
    AT_GREETED, AT_LOADED, AT_NORM, AT_BEGUN, AT_FRONT0, AT_ATT0, AT_ATT1, AT_HID0, AT_GRAD0, AT_OUT0, AT_FIRST, AT_HID1, AT_W2, AT_FRONT1, AT_WA, AT_GRAD1, AT_THIRD, AT_OUT1, AT_W1, AT_LAST, AT_TAIL,
) = range(21)
PLAN = {
    (AT_GREETED, 0): [(D1, REST, 0)],
    (AT_LOADED, 0): [(D0, FIRST, 0), (D1, FIRST, 0), (D0, REST, 0)],
    (AT_NORM, 0): [(D0, HOP, 1), (N0, FIRST, 0), (D0, PAIRS, 0), (N0, REST, 0)],
    (AT_NORM, 1): [QKV, (D0, PAIR_HOP, 1)],
    (AT_BEGUN, 0): [(D0, HOP, 2), (N0, PAIRS, 0), (D0, PAIR_HOP, 2), (N0, HOP, 1), (D0, PAIR_HOP, 3), (N1, REST, 0), (D0, HOP, 3), (D0, OWN, 0), (N0, HOP, 2), (N0, PAIR_HOP, 1), (N1, PAIRS, 0), (N0, PAIR_HOP, 2), (N0, PAIR_HOP, 3), (D1, PAIRS, 0), (D0, OTHER, 0), (N1, PAIR_HOP, 1), (N0, HOP, 3), (D1, HOP, 1), (N0, OWN, 0), (N1, PAIR_HOP, 2), (D1, HOP, 2), (N0, OTHER, 0)],
    (AT_FRONT0, 1): [(N1, PAIR_HOP, 3)],
    (AT_FRONT0, 2): [(N1, FIRST, 0)],
    (AT_FRONT0, 3): [(D1, PAIR_HOP, 1)],
    (AT_ATT0, 0): [(D1, HOP, 3), (D1, PAIR_HOP, 2)],
    (AT_HID0, 0): [(N1, HOP, 1)],
    (AT_HID0, 1): [(D1, PAIR_HOP, 3)],
    (AT_GRAD0, 1): [(N1, HOP, 2)],
    (AT_GRAD0, 3): [(D1, OWN, 0)],
    (AT_OUT0, 1): [(D1, OTHER, 0), (N1, HOP, 3), (N1, OWN, 0)],
    (AT_OUT0, 2): [(G0, CORES, 0), (G0, PAIRS_Z, 3), (G0, OVER_Y, 3), (N1, OTHER, 0), (G0, OVER_Y, 2)],
    (AT_FIRST, 0): [(G0, PAIRS_Z, 2), (G0, ALONG_Z, 3)],
    (AT_HID1, 2): [(O0, CORES, 0), (O0, OVER_Y, 3), (O0, OVER_Y, 2)],
    (AT_HID1, 3): [(O0, PAIRS_Z, 3)],
    (AT_W2, 0): [(G0, ALONG_Z, 2)],
    (AT_W2, 1): [(O0, OVER_Y, 1)],
    (AT_W2, 2): [(G0, PAIRS_Z, 1)],
    (AT_FRONT1, 0): [(G0, OVER_Y, 1)],
    (AT_ATT1, 0): [(O0, ALONG_Z, 3)],
    (AT_ATT1, 2): [(G0, OVER_Y, 0), (O0, ALONG_Z, 2)],
    (AT_ATT1, 3): [(G0, ALONG_Z, 1), (O0, PAIRS_Z, 2)],
    (AT_WA, 1): [(G0, PAIRS_Y, 0), (O0, ALONG_Z, 1)],
    (AT_WA, 2): [(O0, PAIRS_Z, 1), (G0, TOTAL, 0), (O0, OVER_Y, 0)],
    (AT_THIRD, 0): [(O0, PAIRS_Y, 0), (G1, CORES, 0), (G1, PAIRS_Z, 3), (O0, TOTAL, 0), (G1, OVER_Y, 2), (G1, PAIRS_Z, 2), OWNERS],
    (AT_OUT1, 0): [(G1, OVER_Y, 0), (G1, OVER_Y, 3)],
    (AT_W1, 0): [(G1, OVER_Y, 1), (G1, PAIRS_Z, 1), (O1, CORES, 0), (O1, OVER_Y, 3), (G1, ALONG_Z, 3), (O1, OVER_Y, 2)],
    (AT_W1, 1): [(O1, PAIRS_Z, 3)],
    (AT_W1, 2): [(O1, OVER_Y, 0)],
    (AT_W1, 3): [(O1, PAIRS_Z, 2), (O1, OVER_Y, 1), (G1, ALONG_Z, 2), (O1, ALONG_Z, 3)],
    (AT_LAST, 0): [(G1, ALONG_Z, 1), (O1, PAIRS_Z, 1), (O1, ALONG_Z, 2), (G1, PAIRS_Y, 0), (O1, PAIRS_Y, 0)],
    (AT_TAIL, 0): [(O1, ALONG_Z, 1)],
}


def loop(count, tile, at=None, name=None):
    def body(i, carry):
        tile(i)
        for k in range(count):
            if at is not None and (name, k) in PLAN:

                @pl.when(i == k)
                def _():
                    at(name, k)

        return carry

    lax.fori_loop(0, count, body, 0)


def layer_kernel(names, *refs):
    R = SimpleNamespace(**dict(zip(names, refs)))
    width = R.N.shape[-1]
    d, s, z, y, c = place()
    me = d * 16 + s
    partner = (1 - d, s)

    loads = [
        pltpu.make_async_copy(R.x_in, R.x, R.load.at[0]),
        pltpu.make_async_copy(R.dy_in.at[0], R.DY.at[0, z, y, c], R.load.at[1]),
        pltpu.make_async_copy(R.dy_in.at[1], R.DY.at[1, z, y, c], R.load.at[2]),
        pltpu.make_async_copy(R.w1_in, R.W1.at[0], R.load.at[3]),
        pltpu.make_async_copy(R.w2_in, R.W2.at[0], R.load.at[4]),
        pltpu.make_async_copy(R.wd_in, R.Wd.at[d], R.load.at[5]),
    ]
    for copy in loads:
        copy.start()

    cut, cut_out = width * 15 // 16, R.RY.shape[-1]
    D = [Gather(R.dy_in.at[m], R.DY.at[m], R.gather_sem.at[0, m], cut) for m in range(2)]
    N = [Gather(R.N.at[m, z, y, c], R.N.at[m], R.gather_sem.at[1, m], cut) for m in range(2)]

    def scatter(t, m):
        bufs = [R.RC.at[t], R.RY.at[t], R.ZA.at[t], R.ZB.at[t], R.YB.at[t], R.TOT]
        return Scatter((R.PA, R.PB)[t], *bufs, R.scatter_sem.at[t, m], R.free.at[t], m == 1, cut_out)

    O = [scatter(0, m) for m in range(2)]
    G = [scatter(1, m) for m in range(2)]
    small = Exchange(R.pack, R.SG, R.ps, R.pr, True)
    sums = Exchange(R.SG, R.RT, R.ts, R.tr, False)

    steps = {}
    for name, job in ((D0, D[0]), (D1, D[1]), (N0, N[0]), (N1, N[1])):
        for key, step in (
            (REST, job.start_rest), (FIRST, job.start_first), (PAIRS, job.pairs), (OWN, job.own_line), (OTHER, job.other_line),
        ):
            steps[name, key, 0] = step
        for h in (1, 2, 3):
            steps[name, HOP, h] = partial(job.hop, h)
            steps[name, PAIR_HOP, h] = partial(job.pair_hop, h)
    for name, job in ((O0, O[0]), (O1, O[1]), (G0, G[0]), (G1, G[1])):
        steps[name, CORES, 0] = job.cores
        steps[name, PAIRS_Y, 0] = job.pairs_over_y
        for h in (0, 1, 2, 3):
            steps[name, OVER_Y, h] = partial(job.over_y, h)
            steps[name, ALONG_Z, h] = partial(job.along_z, h)
            steps[name, PAIRS_Z, h] = partial(job.pairs_along_z, h)

    def forward_qkv():
        for i in range(3):
            await_bytes(R.Wq.at[3 * d + i], R.qr.at[3 * d + i])
        mine = R.Wq.at[pl.ds(3 * d, 3)]
        send(mine, mine, R.ws.at[3], R.wr.at[3], partner)
        send(R.w1_in, R.W1.at[1], R.ws.at[2], R.wr.at[2], partner)

    steps[QKV] = forward_qkv

    def do(*names):
        for name in names:
            steps[name]()

    def at(place_name, k=0):
        do(*PLAN.get((place_name, k), ()))

    greet_all()
    at(AT_GREETED)
    small.start()
    for i in range(3):
        b = me * 3 + i
        target, entry = b % 16, b // 16

        @pl.when(target == s)
        def _():
            local(R.wq_in.at[i], R.Wq.at[entry], R.qr.at[entry])

        @pl.when(target != s)
        def _():
            send(R.wq_in.at[i], R.Wq.at[entry], R.qs.at[i], R.qr.at[entry], (d, target))

    send(R.wd_in, R.Wd.at[d], R.ws.at[0], R.wr.at[0], partner)
    send(R.w2_in, R.W2.at[1], R.ws.at[1], R.wr.at[1], partner)
    loads[1].wait()
    loads[2].wait()
    at(AT_LOADED)

    R.SG[me] = R.pack[...]
    loads[0].wait()
    small.arrived()
    for j in range(width // 128):
        R.GV[:, 128 * j : 128 * j + 128] = R.SG[2 * j] + R.SG[2 * j + 1]
    gain, shift = R.GV[0:1, :], R.GV[1:2, :]
    for m in range(2):
        rows = R.x[m].astype(F32)
        centred = rows - jnp.mean(rows, 1, keepdims=True)
        rstd = lax.rsqrt(jnp.mean(centred * centred, 1, keepdims=True) + NORM_EPS)
        R.N[m, z, y, c] = (centred * rstd * gain + shift).astype(BF)
        at(AT_NORM, m)
    for p in range(3):
        row = None
        for e in range(2):
            b = s + 16 * (2 * p + e)
            part = R.SG[b // 3, pl.ds(3 + b % 3, 1), :]
            row = part if row is None else row + part
        R.bq[:, 128 * p : 128 * p + 128] = row
    for k in range(2):
        R.b1[:, 128 * k : 128 * k + 128] = R.SG[me, 6 + k : 7 + k, :]
        R.b1[:, 256 + 128 * k : 384 + 128 * k] = R.SG[(1 - d) * 16 + s, 6 + k : 7 + k, :]
    R.gh_sum[...] = jnp.zeros_like(R.gh_sum)
    R.mm_sum[...] = jnp.zeros_like(R.mm_sum)
    R.row_sums[...] = jnp.zeros_like(R.row_sums)

    at(AT_BEGUN)

    D[0].arrived()
    N[0].arrived()
    for copy in loads[3:]:
        copy.wait()
    await_bytes(R.Wd.at[0], R.wr.at[0])
    await_bytes(R.Wq.at[pl.ds(0, 3)], R.wr.at[3])

    def turn(src):
        for m in range(2):
            for i in range(4):
                turn_tile(R, src, m, i)

    stages = [R.stage.at[0], R.stage.at[1]]
    pending = [None, None]

    def keep(value, rows, cols, k):
        if pending[k % 2] is not None:
            pending[k % 2].wait()
        stage = stages[k % 2].at[: value.shape[0], :]
        stage[...] = value
        pending[k % 2] = pltpu.make_async_copy(stage, R.own.at[rows, cols], R.stage_sem.at[k % 2])
        pending[k % 2].start()

    def keep_both(value, lo, cols):
        keep(value[:128], slice(lo, lo + 128), cols, 0)
        keep(value[128:], slice(lo + 128, lo + 256), cols, 1)

    def hidden_grads(src, tokens, lo, sem, name):
        turn(src)
        for k, col in enumerate(range(0, width, 512)):
            cols = slice(col, col + 512)
            total = dot_nn(R.AT[...], tokens[:, :, :, :, :, cols].reshape(8 * QB, 512))
            keep_both(total[:256], lo, cols)
            R.gx[lo : lo + 256, cols] = total[256:].astype(BF)
            at(name, k)
        rows = slice(lo, lo + 256)
        send(R.gx.at[rows], R.RX.at[rows], R.xs.at[sem], R.xr.at[sem], partner)

    def attention_grads():
        turn(R.MM)
        for k, col in enumerate(range(0, width, 512)):
            cols = slice(col, col + 512)
            gq = dot_nn(R.AT[:384, :], R.N[:, :, :, :, :, cols].reshape(8 * QB, 512))
            R.gq[:, :, cols] = gq.astype(BF).reshape(6, 64, 512)
            gd = dot_nn(R.AT[384:, :], R.DY[:, :, :, :, :, cols].reshape(8 * QB, 512))
            keep(jnp.where(d == 0, gd[:64], gd[64:]), slice(512, 576), cols, k)
            R.gx[512:, cols] = jnp.where(d == 0, gd[64:], gd[:64]).astype(BF)
            at(AT_WA, k)
        send(R.gq.at[pl.ds(3 * (1 - d), 3)], R.XB, R.xs.at[0], R.xr.at[0], partner)
        send(R.gx.at[512:], R.RX.at[512:], R.xs.at[1], R.xr.at[1], partner)

    def attention(m):
        limit = R.limits[m : m + 1, :]
        for qb in range(4):
            attention_tile(R, m, qb, limit)
            at((AT_ATT0, AT_ATT1)[m], qb)
        loop(4, partial(key_tile, R, m))

    def finish_out(m):
        total = O[m].total()
        R.hidden_out[m] = (R.x[m].astype(F32) + total + R.GV[2:3, :]).astype(BF)
        if m == 0:
            O[m].release()

    def finish_grad(m):
        total = G[m].total()
        rows = R.x[m].astype(F32)
        centred = rows - jnp.mean(rows, 1, keepdims=True)
        rstd = lax.rsqrt(jnp.mean(centred * centred, 1, keepdims=True) + NORM_EPS)
        xhat = centred * rstd
        g = total * R.GV[0:1, :]
        dy = R.DY[m, z, y, c].astype(F32)
        R.input_grad[m] = dy + rstd * (g - jnp.mean(g, 1, keepdims=True) - xhat * jnp.mean(g * xhat, 1, keepdims=True))
        R.row_sums[0:1, :] += jnp.sum(total * xhat, 0, keepdims=True)
        R.row_sums[1:2, :] += jnp.sum(total, 0, keepdims=True)
        R.row_sums[2:3, :] += jnp.sum(dy, 0, keepdims=True)
        if m == 0:
            G[m].release()

    def to_owners():
        await_bytes(R.XB, R.xr.at[0])
        await_bytes(R.XB, R.xs.at[0])
        for i in range(3):
            b = s + 16 * (3 * d + i)
            owner, where = b // 3 - 16 * d, b % 3
            block = R.gq.at[3 * d + i]
            block[...] = (block[...].astype(F32) + R.XB[i].astype(F32)).astype(BF)

            @pl.when(owner == s)
            def _():
                local(block, R.RQ.at[where], R.rqr.at[where])

            @pl.when(owner != s)
            def _():
                send(block, R.RQ.at[where], R.rqs.at[i], R.rqr.at[where], (d, owner))

    steps.update({(G0, TOTAL, 0): partial(finish_grad, 0), (O0, TOTAL, 0): partial(finish_out, 0), OWNERS: to_owners})
    loop(4, partial(front_tile, R, 0), at, AT_FRONT0)
    attention(0)
    await_bytes(R.W2.at[1], R.wr.at[1])
    await_bytes(R.W1.at[1], R.wr.at[2])
    loop(4, partial(hidden_tile, R, 0), at, AT_HID0)
    loop(4, lambda i: grad_tile(R, 0, i, R.PB), at, AT_GRAD0)
    G[0].start()
    loop(4, lambda i: out_tile(R, 0, i, R.PA), at, AT_OUT0)
    O[0].start()
    at(AT_FIRST)
    D[1].arrived()
    N[1].arrived()
    loop(4, partial(hidden_tile, R, 1), at, AT_HID1)
    hidden_grads(R.ACT, R.DY, 0, 2, AT_W2)
    loop(4, partial(front_tile, R, 1), at, AT_FRONT1)
    attention(1)
    attention_grads()
    G[0].drain()
    loop(4, lambda i: grad_tile(R, 1, i, R.PB), at, AT_GRAD1)
    G[1].start()
    at(AT_THIRD)
    O[0].drain()
    loop(4, lambda i: out_tile(R, 1, i, R.PA), at, AT_OUT1)
    O[1].start()
    hidden_grads(R.GH, R.N, 256, 3, AT_W1)
    at(AT_LAST)
    finish_grad(1)
    R.SG[...] = jnp.zeros_like(R.SG)
    for owner in range(32):
        block = slice(128 * (owner // 2), 128 * (owner // 2) + 128)
        R.SG[owner, 0:3, :] = R.row_sums[0:3, block]
    lane_half = head_lanes((1, 128), 1)
    for j in range(6):
        b = s + 16 * j
        row = R.mm_sum[:, 128 * (j // 2) : 128 * (j // 2) + 128]
        R.SG[b // 3, pl.ds(3 + b % 3, 1), :] = jnp.where(lane_half == j % 2, row, 0.0)
    for k in range(2):
        R.SG[me, 6 + k : 7 + k, :] = R.gh_sum[:, 128 * k : 128 * k + 128]
        R.SG[(1 - d) * 16 + s, 6 + k : 7 + k, :] = R.gh_sum[:, 256 + 128 * k : 384 + 128 * k]
    sums.start()
    R.RT[me] = R.SG[me]
    at(AT_TAIL)
    sums.arrived()
    R.small_out[...] = jnp.sum(R.RT[...], 0)
    finish_out(1)

    for i in range(3):
        await_bytes(R.RQ.at[i], R.rqr.at[i])
        b = s + 16 * (3 * d + i)

        @pl.when(b // 3 - 16 * d != s)
        def _():
            await_bytes(R.gq.at[i], R.rqs.at[i])

        @pl.when((me * 3 + i) % 16 != s)
        def _():
            await_bytes(R.wq_in.at[i], R.qs.at[i])

    for k, rows in ((1, slice(512, 576)), (2, slice(0, 256)), (3, slice(256, 512))):
        await_bytes(R.gx.at[rows], R.xs.at[k])
        await_bytes(R.RX.at[rows], R.xr.at[k])
    await_bytes(R.Wd.at[0], R.ws.at[0])
    await_bytes(R.W2.at[0], R.ws.at[1])
    await_bytes(R.W1.at[0], R.ws.at[2])
    await_bytes(R.Wq.at[pl.ds(0, 3)], R.ws.at[3])
    for copy in pending:
        copy.wait()
    for job in D + N + [O[1], G[1], small, sums]:
        job.drain()


def run_layer(pack, x, dy, wq, wd, w1, w2, cos, sin, limits):
    width = x.shape[-1]
    vm = pl.BlockSpec(memory_space=pltpu.VMEM)
    hbm = pl.BlockSpec(memory_space=pl.ANY)
    dma = pltpu.SemaphoreType.DMA
    names = ["pack", "x_in", "dy_in", "wq_in", "wd_in", "w1_in", "w2_in", "cos", "sin", "limits"]
    names += ["hidden_out", "input_grad", "small_out", "own", "RX", "RQ"]

    def low(*shape):
        return pltpu.VMEM(shape, BF)

    def wide(*shape):
        return pltpu.VMEM(shape, F32)

    chunks = (4, 2, 2, 64, width)
    cut = width * 13 // 16
    scratch = dict(
        N=low(2, *chunks), DY=low(2, *chunks), x=low(2, 64, width),
        Wq=low(6, 64, width), Wd=low(2, 64, width), W1=low(2, 256, width), W2=low(2, 256, width),
        SG=wide(32, 8, 128), GV=wide(8, width), bq=wide(1, 384), b1=wide(1, 512),
        Q=low(1024, 128), K=low(1024, 128), V=low(1024, 128), GM=low(1024, 128),
        KT=low(4, 128, QB), VT=low(4, 128, QB),
        ACT=low(2, 1024, 512), GH=low(2, 1024, 512), MM=low(2, 1024, 512), AT=low(512, 2048),
        DK=wide(1024, 128), DV=wide(1024, 128),
        PA=low(*chunks), PB=low(*chunks),
        RC=low(2, 4, 2, 64, width), RY=low(2, 4, 64, cut), ZA=low(2, 5, 64, cut), ZB=low(2, 5, 2, 64, max(128, width - cut)),
        YB=low(2, 64, max(128, width - cut)), TOT=wide(64, width),
        gq=low(6, 64, width), gx=low(576, width), XB=low(3, 64, width), stage=wide(2, 128, 512),
        gh_sum=wide(1, 512), mm_sum=wide(1, 384), row_sums=wide(8, width), RT=wide(32, 8, 128),
        load=dma((6,)), gather_sem=dma((2, 2, Gather.SEMS)), scatter_sem=dma((2, 2, Scatter.SEMS)),
        free=pltpu.SemaphoreType.REGULAR((2, 4)),
        ps=dma((1,)), pr=dma((1,)), ts=dma((1,)), tr=dma((1,)),
        qs=dma((3,)), qr=dma((6,)), ws=dma((4,)), wr=dma((4,)), xs=dma((4,)), xr=dma((4,)), rqs=dma((3,)), rqr=dma((3,)),
        stage_sem=dma((2,)),
    )
    return pl.pallas_call(
        partial(layer_kernel, names + list(scratch)),
        name="layer",
        out_shape=(
            jax.ShapeDtypeStruct((2, 64, width), BF),
            jax.ShapeDtypeStruct((2, 64, width), F32),
            jax.ShapeDtypeStruct((8, 128), F32),
            jax.ShapeDtypeStruct((576, width), F32),
            jax.ShapeDtypeStruct((576, width), BF),
            jax.ShapeDtypeStruct((3, 64, width), BF),
        ),
        in_specs=[vm] + [hbm] * 6 + [vm, vm, vm],
        out_specs=(vm, vm, vm, hbm, hbm, hbm),
        scratch_shapes=list(scratch.values()),
        compiler_params=pltpu.CompilerParams(collective_id=0, has_side_effects=True, vmem_limit_bytes=250 * 2**18),
    )(pack, x, dy, wq.reshape(3, 64, width), wd, w1, w2, cos, sin, limits)


def finish_kernel(own, RX, RQ, hidden_in, input_in, qkv, dense, fc1, fc2, hidden_out, input_grad):
    qkv[...] = RQ[...].reshape(qkv.shape).astype(F32)
    fc2[...] = own[:256, :] + RX[:256, :].astype(F32)
    fc1[...] = own[256:512, :] + RX[256:512, :].astype(F32)
    dense[...] = own[512:, :] + RX[512:, :].astype(F32)
    hidden_out[...] = hidden_in[...]
    input_grad[...] = input_in[...]


def run_finish(own, RX, RQ, hidden_out, input_grad):
    width = own.shape[1]
    part = width // 4

    def rows(count):
        return pl.BlockSpec((count, part), lambda i: (0, i))

    def cube(a, b):
        return pl.BlockSpec((a, b, part), lambda i: (0, 0, i))

    return pl.pallas_call(
        finish_kernel,
        name="finish",
        grid=(4,),
        out_shape=(
            jax.ShapeDtypeStruct((192, width), F32),
            jax.ShapeDtypeStruct((64, width), F32),
            jax.ShapeDtypeStruct((256, width), F32),
            jax.ShapeDtypeStruct((256, width), F32),
            jax.ShapeDtypeStruct(hidden_out.shape, BF),
            jax.ShapeDtypeStruct(input_grad.shape, F32),
        ),
        in_specs=[rows(576), rows(576), cube(3, 64), cube(2, 64), cube(2, 64)],
        out_specs=(rows(192), rows(64), rows(256), rows(256), cube(2, 64), cube(2, 64)),
        compiler_params=pltpu.CompilerParams(vmem_limit_bytes=250 * 2**18),
    )(own, RX, RQ, hidden_out, input_grad)


def rotary_rows(length):
    half_rot = ROT // 2
    frequency = np.power(np.float32(10000.0), -np.arange(half_rot, dtype=np.float32) * np.float32(2.0) / np.float32(ROT))
    angles = np.arange(length, dtype=np.float32)[:, None] * frequency.astype(np.float32)[None, :]
    cosine, sine = np.cos(angles), np.sin(angles)
    rest = np.zeros((length, HEAD - ROT), np.float32)
    cosine = np.concatenate([cosine, cosine, rest + 1.0], 1)
    sine = np.concatenate([-sine, sine, rest], 1)
    return np.tile(cosine, (1, 2)).astype(np.float32), np.tile(sine, (1, 2)).astype(np.float32)


def by_heads(
    hidden_in, cotangent, prefix_len, qkv_weight, dense_weight, fc1_weight, fc2_weight,
    norm_gain, norm_shift, qkv_bias, dense_bias, fc1_bias, fc2_bias,
):
    width = hidden_in.shape[-1]
    d, s, z, y, c = place()
    me = d * 16 + s

    def beside(rows, right):
        right = jnp.reshape(right, (-1, 1))
        return jnp.concatenate([jnp.where(right, 0.0, rows), jnp.where(right, rows, 0.0)], 1)

    thirds = jnp.stack([norm_gain, norm_shift, dense_bias]).astype(F32).at[2].add(fc2_bias.astype(F32))
    pack = jnp.concatenate(
        [
            beside(thirds, me % 2 == 1),
            beside(qkv_bias.astype(F32).reshape(3, 64), ((me * 3 + jnp.arange(3)) // 16) % 2 == 1),
            fc1_bias.astype(F32).reshape(2, 128),
        ],
        0,
    )
    cos, sin = rotary_rows(hidden_in.shape[2] * 16)
    hidden_out, input_grad, small, own, RX, RQ = run_layer(
        pack, hidden_in.reshape(2, 64, width), cotangent.reshape(2, 64, width),
        qkv_weight, dense_weight, fc1_weight, fc2_weight, cos, sin, prefix_len,
    )
    qkv_grad, dense_grad, fc1_grad, fc2_grad, hidden_out, input_grad = run_finish(own, RX, RQ, hidden_out, input_grad)
    thirds = jnp.where(me % 2 == 1, small[:3, 64:], small[:3, :64])
    return (
        hidden_out.reshape(hidden_in.shape),
        input_grad.reshape(hidden_in.shape),
        qkv_grad,
        dense_grad,
        fc1_grad,
        fc2_grad,
        thirds[0],
        thirds[1],
        (small[3:6, :64] + small[3:6, 64:]).reshape(192),
        thirds[2],
        small[6:8].reshape(256),
        thirds[2],
    )


def solution(mesh):
    in_specs = (
        P(None, "dp", "seq", None),
        P(None, "dp", "seq", None),
        P(None, "dp"),
        P(("dp", "seq"), None),
        P(("dp", "seq"), None),
        P(("dp", "seq"), None),
        P(("dp", "seq"), None),
        P(("dp", "seq")),
        P(("dp", "seq")),
        P(("dp", "seq")),
        P(("dp", "seq")),
        P(("dp", "seq")),
        P(("dp", "seq")),
    )
    out_specs = (
        P(None, "dp", "seq", None),
        P(None, "dp", "seq", None),
        P(("dp", "seq"), None),
        P(("dp", "seq"), None),
        P(("dp", "seq"), None),
        P(("dp", "seq"), None),
        P(("dp", "seq")),
        P(("dp", "seq")),
        P(("dp", "seq")),
        P(("dp", "seq")),
        P(("dp", "seq")),
        P(("dp", "seq")),
    )
    fits = mesh.shape["dp"] == 2 and mesh.shape["seq"] == 16

    def body(*args):
        return (by_heads if fits and args[0].shape[0] == 2 and args[0].shape[2] == 64 else on_device)(*args)

    return jax.shard_map(
        body, mesh=mesh, in_specs=in_specs, out_specs=out_specs, check_vma=False
    )
```

```python
from functools import partial
import math
from types import SimpleNamespace

import jax
import jax.numpy as jnp
import numpy as np
from jax import lax
from jax.experimental import pallas as pl
from jax.experimental.pallas import tpu as pltpu
from jax.sharding import PartitionSpec as P

HEADS = 32
HEAD = 64
ROT = 32


NORM_EPS = 1e-05
MASKED_LOW = -1e30
TANH_FACTOR = 0.7978845608028654
CUBIC_FACTOR = 0.044715


def gelu_tanh(inputs_in):
    return (
        0.5
        * inputs_in
        * (
            1.0
            + jnp.tanh(TANH_FACTOR * (inputs_in + CUBIC_FACTOR * inputs_in * inputs_in * inputs_in))
        )
    )


def rotary_tables(first_place, length):
    half_rot = ROT // 2
    frequency = jnp.power(10000.0, -jnp.arange(half_rot).astype(jnp.float32) * 2.0 / ROT)
    places = (first_place + jnp.arange(length, dtype=jnp.int32)).astype(jnp.float32)
    angles = places[:, None] * frequency[None, :]
    angles = jnp.concatenate([angles, angles], 1)
    return (jnp.cos(angles)[:, None, :], jnp.sin(angles)[:, None, :])


def rotate(head_view, cosine, sine):
    half_rot = ROT // 2
    turned = head_view[..., :ROT]
    swapped = jnp.concatenate([-turned[..., half_rot:], turned[..., :half_rot]], -1)
    return jnp.concatenate([turned * cosine + swapped * sine, head_view[..., ROT:]], -1)


def norm_apply(tokens, scale_gain, shift_bias):
    centred = tokens - jnp.mean(tokens, 1, keepdims=True)
    rstd = lax.rsqrt(jnp.mean(centred * centred, 1, keepdims=True) + NORM_EPS)
    return centred * rstd * scale_gain + shift_bias


def contract_last(left, right):
    return lax.dot_general(
        left, right, (((1,), (1,)), ((), ())), preferred_element_type=jnp.float32
    )


def visible_mask(query_places, key_places, limits):
    reach = jnp.maximum(query_places[None, :], limits[:, None] - 1)
    return (key_places[None, None, :] <= reach[:, :, None])[:, None]


def forward_part(tokens, limits, params, first_place, cosine, sine):
    (
        qkv_weight,
        dense_weight,
        fc1_weight,
        fc2_weight,
        norm_gain,
        norm_shift,
        qkv_bias,
        dense_bias,
        fc1_bias,
        fc2_bias,
    ) = params
    seq_count, local_len, model_width = tokens.shape
    score_scale = 1.0 / math.sqrt(HEAD)
    flat_rows = tokens.reshape(seq_count * local_len, model_width).astype(jnp.float32)
    normed_low = norm_apply(
        flat_rows, norm_gain.astype(jnp.float32), norm_shift.astype(jnp.float32)
    ).astype(jnp.bfloat16)
    merged = contract_last(normed_low, qkv_weight) + qkv_bias.astype(jnp.float32)
    head_view = merged.reshape(seq_count, local_len, 3, HEADS, HEAD)
    query_low = rotate(head_view[:, :, 0], cosine, sine).astype(jnp.bfloat16)
    key_low = (
        rotate(head_view[:, :, 1], cosine, sine)
        .astype(jnp.bfloat16)
        .reshape(seq_count, local_len, model_width)
    )
    value_low = head_view[:, :, 2].astype(jnp.bfloat16).reshape(seq_count, local_len, model_width)
    query_places = first_place + jnp.arange(local_len, dtype=jnp.int32)
    row_top = jnp.full((seq_count, HEADS, local_len), MASKED_LOW, jnp.float32)
    keys_piece = lax.all_gather(key_low, "seq", axis=1, tiled=True)
    values_piece = lax.all_gather(value_low, "seq", axis=1, tiled=True)
    piece_len = keys_piece.shape[1]
    keys_piece = keys_piece.reshape(seq_count, piece_len, HEADS, HEAD)
    values_piece = values_piece.reshape(seq_count, piece_len, HEADS, HEAD)
    scores = (
        jnp.einsum("sqhd,skhd->shqk", query_low, keys_piece, preferred_element_type=jnp.float32)
        * score_scale
    )
    visible = visible_mask(query_places, jnp.arange(piece_len, dtype=jnp.int32), limits)
    masked = jnp.where(visible, scores, MASKED_LOW)
    new_top = jnp.maximum(row_top, jnp.max(masked, -1))
    exp_weights = jnp.where(visible, jnp.exp(masked - new_top[..., None]), 0.0)
    row_total = jnp.sum(exp_weights, -1)
    accum = jnp.einsum(
        "shqk,skhd->shqd",
        exp_weights.astype(jnp.bfloat16),
        values_piece,
        preferred_element_type=jnp.float32,
    )
    row_top, row_total, accum = (new_top, row_total, accum)
    mixed = accum / row_total[..., None]
    log_total = row_top + jnp.log(row_total)
    mixed_low = (
        mixed.transpose(0, 2, 1, 3).reshape(seq_count * local_len, model_width).astype(jnp.bfloat16)
    )
    hidden_pre = contract_last(normed_low, fc1_weight) + fc1_bias.astype(jnp.float32)
    act_low = gelu_tanh(hidden_pre).astype(jnp.bfloat16)
    result = (
        flat_rows
        + jnp.dot(mixed_low, dense_weight, preferred_element_type=jnp.float32)
        + dense_bias.astype(jnp.float32)
    )
    result = (
        result
        + jnp.dot(act_low, fc2_weight, preferred_element_type=jnp.float32)
        + fc2_bias.astype(jnp.float32)
    )
    saved_parts = (
        flat_rows,
        normed_low,
        query_low,
        key_low,
        value_low,
        mixed,
        log_total,
        hidden_pre,
        act_low,
        mixed_low,
    )
    return (result.astype(jnp.bfloat16).reshape(tokens.shape), saved_parts)


def backward_part(grad_low, limits, params, first_place, cosine, sine, saved_parts):
    (
        qkv_weight,
        dense_weight,
        fc1_weight,
        fc2_weight,
        norm_gain,
        norm_shift,
        qkv_bias,
        dense_bias,
        fc1_bias,
        fc2_bias,
    ) = params
    (
        flat_rows,
        normed_low,
        query_low,
        key_low,
        value_low,
        mixed,
        log_total,
        hidden_pre,
        act_low,
        mixed_low,
    ) = saved_parts
    seq_count, local_len, model_width = grad_low.shape
    score_scale = 1.0 / math.sqrt(HEAD)
    grad_rows_low = grad_low.reshape(seq_count * local_len, model_width)
    grad_rows = grad_rows_low.astype(jnp.float32)
    grad_mixed_low = contract_last(grad_rows_low, dense_weight).astype(jnp.bfloat16)
    grad_act = contract_last(grad_rows_low, fc2_weight)
    gelu_pull = jax.vjp(gelu_tanh, hidden_pre)[1]
    grad_hidden_low = gelu_pull(grad_act)[0].astype(jnp.bfloat16)
    grad_out_heads = grad_mixed_low.reshape(seq_count, local_len, HEADS, HEAD)
    delta = jnp.sum(grad_out_heads.astype(jnp.float32).transpose(0, 2, 1, 3) * mixed, -1)
    stats_lse, stats_delta = (
        lax.all_gather(log_total.transpose(0, 2, 1), "seq", axis=1, tiled=True),
        lax.all_gather(delta.transpose(0, 2, 1), "seq", axis=1, tiled=True),
    )
    local_places = first_place + jnp.arange(local_len, dtype=jnp.int32)
    key_heads = key_low.reshape(seq_count, local_len, HEADS, HEAD)
    value_heads = value_low.reshape(seq_count, local_len, HEADS, HEAD)
    keys_piece = lax.all_gather(key_low, "seq", axis=1, tiled=True)
    values_piece = lax.all_gather(value_low, "seq", axis=1, tiled=True)
    piece_len = keys_piece.shape[1]
    keys_piece = keys_piece.reshape(seq_count, piece_len, HEADS, HEAD)
    values_piece = values_piece.reshape(seq_count, piece_len, HEADS, HEAD)
    scores = (
        jnp.einsum("sqhd,skhd->shqk", query_low, keys_piece, preferred_element_type=jnp.float32)
        * score_scale
    )
    visible = visible_mask(local_places, jnp.arange(piece_len, dtype=jnp.int32), limits)
    prob_rows = jnp.where(visible, jnp.exp(scores - log_total[..., None]), 0.0)
    grad_probs = jnp.einsum(
        "sqhd,skhd->shqk", grad_out_heads, values_piece, preferred_element_type=jnp.float32
    )
    grad_scores = (prob_rows * (grad_probs - delta[..., None])).astype(jnp.bfloat16)
    grad_query = score_scale * jnp.einsum(
        "shqk,skhd->sqhd", grad_scores, keys_piece, preferred_element_type=jnp.float32
    )
    query_flat = query_low.reshape(seq_count, local_len, model_width)
    grad_out_flat = grad_mixed_low.reshape(seq_count, local_len, model_width)
    queries_piece = lax.all_gather(query_flat, "seq", axis=1, tiled=True)
    grad_out_piece = lax.all_gather(grad_out_flat, "seq", axis=1, tiled=True)
    piece_len = queries_piece.shape[1]
    queries_piece = queries_piece.reshape(seq_count, piece_len, HEADS, HEAD)
    grad_out_piece = grad_out_piece.reshape(seq_count, piece_len, HEADS, HEAD)
    piece_lse = stats_lse.transpose(0, 2, 1)
    piece_delta = stats_delta.transpose(0, 2, 1)
    scores = (
        jnp.einsum("sqhd,skhd->shqk", queries_piece, key_heads, preferred_element_type=jnp.float32)
        * score_scale
    )
    visible = visible_mask(jnp.arange(piece_len, dtype=jnp.int32), local_places, limits)
    prob_rows = jnp.where(visible, jnp.exp(scores - piece_lse[..., None]), 0.0)
    grad_probs = jnp.einsum(
        "sqhd,skhd->shqk", grad_out_piece, value_heads, preferred_element_type=jnp.float32
    )
    grad_scores = (prob_rows * (grad_probs - piece_delta[..., None])).astype(jnp.bfloat16)
    grad_values = jnp.einsum(
        "shqk,sqhd->skhd",
        prob_rows.astype(jnp.bfloat16),
        grad_out_piece,
        preferred_element_type=jnp.float32,
    )
    grad_keys = score_scale * jnp.einsum(
        "shqk,sqhd->skhd", grad_scores, queries_piece, preferred_element_type=jnp.float32
    )
    grad_keys, grad_values = (grad_keys, grad_values)
    paired = jnp.stack([grad_query, grad_keys], 0)
    rotate_pull = jax.vjp(partial(rotate, cosine=cosine, sine=sine), paired)[1]
    unturned = rotate_pull(paired)[0]
    grad_merged_low = (
        jnp.stack([unturned[0], unturned[1], grad_values], 2)
        .reshape(seq_count * local_len, 3 * model_width)
        .astype(jnp.bfloat16)
    )
    grad_normed = jnp.dot(
        grad_merged_low, qkv_weight, preferred_element_type=jnp.float32
    ) + jnp.dot(grad_hidden_low, fc1_weight, preferred_element_type=jnp.float32)
    norm_pull = jax.vjp(
        norm_apply, flat_rows, norm_gain.astype(jnp.float32), norm_shift.astype(jnp.float32)
    )[1]
    grad_flat, grad_gain, grad_shift = norm_pull(grad_normed)
    input_grad = (grad_rows + grad_flat).reshape(seq_count, local_len, model_width)
    bias_sums = jnp.sum(grad_rows, 0)
    small_terms = (
        grad_gain,
        grad_shift,
        jnp.sum(grad_merged_low.astype(jnp.float32), 0),
        bias_sums,
        jnp.sum(grad_hidden_low.astype(jnp.float32), 0),
        bias_sums,
    )
    operand_set = (normed_low, grad_merged_low, mixed_low, grad_rows_low, grad_hidden_low, act_low)
    return (input_grad, small_terms, operand_set)


def terms_builder(operand_set, row_sizes, model_width, row_count):
    normed_all, grad_merged_all, mixed_all, grad_out_all, grad_hidden_all, act_all = operand_set
    rows_qkv, rows_dense, rows_fc1, rows_fc2 = row_sizes
    block_rows = rows_qkv + rows_dense + rows_fc1 + rows_fc2
    block_count = row_count // block_rows

    def outer_term(left, right, block_width):
        term = lax.dot_general(
            left, right, (((0,), (0,)), ((), ())), preferred_element_type=jnp.float32
        )
        return term.reshape(block_count, block_width, model_width)

    term_parts = [
        outer_term(grad_merged_all, normed_all, rows_qkv),
        outer_term(mixed_all, grad_out_all, rows_dense),
        outer_term(grad_hidden_all, normed_all, rows_fc1),
        outer_term(act_all, grad_out_all, rows_fc2),
    ]
    return jnp.concatenate(term_parts, 1).reshape(row_count, model_width)


def on_device(
    hidden_in,
    cotangent,
    prefix_len,
    qkv_weight,
    dense_weight,
    fc1_weight,
    fc2_weight,
    norm_gain,
    norm_shift,
    qkv_bias,
    dense_bias,
    fc1_bias,
    fc2_bias,
):
    micro_count, seq_count, local_len, model_width = hidden_in.shape
    first_place = lax.axis_index("seq") * local_len
    cosine, sine = rotary_tables(first_place, local_len)
    row_sizes = (
        qkv_weight.shape[0],
        dense_weight.shape[0],
        fc1_weight.shape[0],
        fc2_weight.shape[0],
    )
    block_rows = row_sizes[0] + row_sizes[1] + row_sizes[2] + row_sizes[3]
    params = (
        lax.all_gather(qkv_weight, ("dp", "seq"), axis=0, tiled=True),
        lax.all_gather(dense_weight, ("dp", "seq"), axis=0, tiled=True),
        lax.all_gather(fc1_weight, ("dp", "seq"), axis=0, tiled=True),
        lax.all_gather(fc2_weight, ("dp", "seq"), axis=0, tiled=True),
        lax.all_gather(norm_gain, ("dp", "seq"), axis=0, tiled=True),
        lax.all_gather(norm_shift, ("dp", "seq"), axis=0, tiled=True),
        lax.all_gather(qkv_bias, ("dp", "seq"), axis=0, tiled=True),
        lax.all_gather(dense_bias, ("dp", "seq"), axis=0, tiled=True),
        lax.all_gather(fc1_bias, ("dp", "seq"), axis=0, tiled=True),
        lax.all_gather(fc2_bias, ("dp", "seq"), axis=0, tiled=True),
    )
    outputs = []
    input_grads = []
    small_totals = None
    operand_lists = []
    weight_rows = None
    for batch_index in range(micro_count):
        limits = prefix_len[batch_index]
        result, saved_parts = forward_part(
            hidden_in[batch_index], limits, params, first_place, cosine, sine
        )
        input_grad, small_terms, operand_set = backward_part(
            cotangent[batch_index], limits, params, first_place, cosine, sine, saved_parts
        )
        outputs.append(result)
        input_grads.append(input_grad)
        operand_lists.append(operand_set)
        if small_totals is None:
            small_totals = small_terms
        else:
            small_totals = tuple(
                (old_sum + new_term for old_sum, new_term in zip(small_totals, small_terms))
            )
    joined_set = tuple(
        (jnp.concatenate([entry[place] for entry in operand_lists], 0) for place in range(6))
    )
    weight_rows = lax.psum_scatter(
        terms_builder(
            joined_set, row_sizes, model_width, block_rows * lax.axis_size(("dp", "seq"))
        ),
        ("dp", "seq"),
        scatter_dimension=0,
        tiled=True,
    )
    rows_qkv, rows_dense, rows_fc1, rows_fc2 = row_sizes
    qkv_grad = weight_rows[:rows_qkv]
    dense_grad = weight_rows[rows_qkv : rows_qkv + rows_dense]
    fc1_grad = weight_rows[rows_qkv + rows_dense : rows_qkv + rows_dense + rows_fc1]
    fc2_grad = weight_rows[rows_qkv + rows_dense + rows_fc1 :]
    gain_grad, shift_grad, qkv_bias_grad, dense_bias_grad, fc1_bias_grad, fc2_bias_grad = (
        lax.psum_scatter(small_totals[0], ("dp", "seq"), scatter_dimension=0, tiled=True),
        lax.psum_scatter(small_totals[1], ("dp", "seq"), scatter_dimension=0, tiled=True),
        lax.psum_scatter(small_totals[2], ("dp", "seq"), scatter_dimension=0, tiled=True),
        lax.psum_scatter(small_totals[3], ("dp", "seq"), scatter_dimension=0, tiled=True),
        lax.psum_scatter(small_totals[4], ("dp", "seq"), scatter_dimension=0, tiled=True),
        lax.psum_scatter(small_totals[5], ("dp", "seq"), scatter_dimension=0, tiled=True),
    )
    return (
        jnp.stack(outputs, 0),
        jnp.stack(input_grads, 0),
        qkv_grad,
        dense_grad,
        fc1_grad,
        fc2_grad,
        gain_grad,
        shift_grad,
        qkv_bias_grad,
        dense_bias_grad,
        fc1_bias_grad,
        fc2_bias_grad,
    )


MESH = pl.DeviceIdType.MESH
BF = jnp.bfloat16
F32 = jnp.float32


def place():
    d = lax.axis_index("dp")
    s = lax.axis_index("seq")
    return d, s, s // 4, (s // 2) % 2, s % 2


def seq_of(z, y, c):
    return z * 4 + y * 2 + c


def send(src, dst, ssem, rsem, target):
    pltpu.make_async_remote_copy(
        src_ref=src, dst_ref=dst, send_sem=ssem, recv_sem=rsem, device_id=target, device_id_type=MESH
    ).start()


def local(src, dst, sem):
    pltpu.make_async_copy(src, dst, sem).start()


def await_bytes(ref, sem):
    pltpu.make_async_copy(ref, ref, sem).wait()


def signal(sem, target):
    pl.semaphore_signal(sem, inc=1, device_id=target, device_id_type=MESH)


class Gather:
    SEMS = 38

    def __init__(self, src, G, sem, cut):
        self.src, self.G, self.sem, self.cut, self.width = src, G, sem, cut, G.shape[-1]

    def first(self, zz, yy):
        d, s, z, y, c = place()
        return self.G.at[zz, yy, c, :, slice(0, self.cut)]

    def pair(self, zz):
        d, s, z, y, c = place()
        return self.G.at[zz, :, c, :, slice(self.cut, self.width)]

    def along_z(self, src, dst, up, down, recv, to_up, to_down):
        d, s, z, y, c = place()
        if to_up:

            @pl.when(z < 3)
            def _():
                send(src, dst, self.sem.at[up], self.sem.at[recv], (d, s + 4))

        if to_down:

            @pl.when(z > 0)
            def _():
                send(src, dst, self.sem.at[down], self.sem.at[recv], (d, s - 4))

    def start_rest(self):
        d, s, z, y, c = place()
        rest = slice(self.cut, self.width)
        over = (d, seq_of(z, 1 - y, c))
        send(self.src.at[:, rest], self.G.at[z, y, c, :, rest], self.sem.at[32], self.sem.at[33], over)

    def start_first(self):
        d, s, z, y, c = place()
        src = self.src.at[:, slice(0, self.cut)]
        self.along_z(src, self.first(z, y), 4 + z, 0 + z, 8 + z, True, True)
        over = (d, seq_of(z, 1 - y, c))
        send(src, self.first(z, y), self.sem.at[24 + z], self.sem.at[28 + z], over)

    def pairs(self):
        d, s, z, y, c = place()
        await_bytes(self.G.at[z, 1 - y, c, :, slice(self.cut, self.width)], self.sem.at[33])
        self.along_z(self.pair(z), self.pair(z), 16 + z, 12 + z, 20 + z, True, True)

    def hop(self, h):
        d, s, z, y, c = place()
        for below in (True, False):
            zz = z - h if below else z + h

            @pl.when(z >= h if below else z + h <= 3)
            def _():
                chunk = self.first(zz, y)
                await_bytes(chunk, self.sem.at[8 + zz])
                self.along_z(chunk, chunk, 4 + zz, 0 + zz, 8 + zz, below, not below)
                send(chunk, chunk, self.sem.at[24 + zz], self.sem.at[28 + zz], (d, seq_of(z, 1 - y, c)))

    def pair_hop(self, h):
        d, s, z, y, c = place()
        for below in (True, False):
            zz = z - h if below else z + h

            @pl.when(z >= h if below else z + h <= 3)
            def _():
                chunk = self.pair(zz)
                await_bytes(chunk, self.sem.at[20 + zz])
                self.along_z(chunk, chunk, 16 + zz, 12 + zz, 20 + zz, below, not below)

    def own_line(self):
        d, s, z, y, c = place()
        line = self.G.at[:, y, c]
        send(line, line, self.sem.at[34], self.sem.at[36], (d, seq_of(z, y, 1 - c)))

    def other_line(self):
        d, s, z, y, c = place()
        for zz in range(4):
            await_bytes(self.first(zz, 1 - y), self.sem.at[28 + zz])
        line = self.G.at[:, 1 - y, c]
        send(line, line, self.sem.at[35], self.sem.at[37], (d, seq_of(z, y, 1 - c)))

    def arrived(self):
        for k in range(2):
            await_bytes(self.G.at[:, 0, 0], self.sem.at[36 + k])

    def drain(self):
        d, s, z, y, c = place()
        await_bytes(self.pair(0).at[0], self.sem.at[32])
        for zz in range(4):
            await_bytes(self.first(0, 0), self.sem.at[24 + zz])

            @pl.when((z < 3) & (zz <= z))
            def _():
                await_bytes(self.first(0, 0), self.sem.at[4 + zz])
                await_bytes(self.pair(0), self.sem.at[16 + zz])

            @pl.when((z > 0) & (zz >= z))
            def _():
                await_bytes(self.first(0, 0), self.sem.at[0 + zz])
                await_bytes(self.pair(0), self.sem.at[12 + zz])

        for k in range(2):
            await_bytes(self.G.at[:, 0, 0], self.sem.at[34 + k])


class Scatter:
    SEMS = 32

    def __init__(self, P, RC, RY, ZA, ZB, YB, TOT, sem, free, reuse, cut):
        self.P, self.RC, self.RY, self.ZA, self.ZB, self.YB, self.TOT = P, RC, RY, ZA, ZB, YB, TOT
        self.sem, self.free, self.reuse, self.cut = sem, free, reuse, cut
        self.head, self.rest = slice(0, cut), slice(cut, P.shape[-1])

    def start(self):
        d, s, z, y, c = place()
        if self.reuse:
            pl.semaphore_wait(self.free.at[0], 1)
        for k, row in ((0, 1 - y), (1, y)):
            send(
                self.P.at[:, row, 1 - c], self.RC.at[:, row], self.sem.at[k], self.sem.at[2 + k], (d, seq_of(z, y, 1 - c))
            )

    def cores(self):
        d, s, z, y, c = place()
        await_bytes(self.RC.at[:, 0], self.sem.at[2])
        await_bytes(self.RC.at[:, 0], self.sem.at[3])
        if self.reuse:
            pl.semaphore_wait(self.free.at[1], 1)

            @pl.when(z < 3)
            def _():
                pl.semaphore_wait(self.free.at[2], 1)

            @pl.when(z > 0)
            def _():
                pl.semaphore_wait(self.free.at[3], 1)

    def targets(self, h, act):
        d, s, z, y, c = place()
        for below in (True, False):
            zz = z - h if below else z + h

            @pl.when(z >= h if below else z + h <= 3)
            def _():
                act(below, zz)

    def over_y(self, h):
        d, s, z, y, c = place()

        def one(below, zz):
            chunk = self.P.at[zz, 1 - y, c, :, self.head]
            chunk[...] = (chunk[...].astype(F32) + self.RC[zz, 1 - y, :, self.head].astype(F32)).astype(BF)
            send(chunk, self.RY.at[zz], self.sem.at[4 + zz], self.sem.at[8 + zz], (d, seq_of(z, 1 - y, c)))

        if h == 0:
            one(True, z)
        else:
            self.targets(h, one)

    def add_beyond(self, chunk, Z, sems, below, zz):
        d, s, z, y, c = place()

        @pl.when(z < 3 if below else z > 0)
        def _():
            await_bytes(Z.at[zz], self.sem.at[sems + zz])
            chunk[...] = (chunk[...].astype(F32) + Z[zz].astype(F32)).astype(BF)

    def pass_on(self, chunk, Z, ssem, sems, below, zz, h):
        d, s, z, y, c = place()
        slot = 4 if h == 1 and not below else zz
        target = (d, s - 4) if below else (d, s + 4)
        send(chunk, Z.at[slot], self.sem.at[ssem + zz], self.sem.at[sems + slot], target)

    def along_z(self, h):
        d, s, z, y, c = place()

        def one(below, zz):
            await_bytes(self.RY.at[zz], self.sem.at[8 + zz])
            chunk = self.P.at[zz, y, c, :, self.head]
            chunk[...] = (
                chunk[...].astype(F32) + self.RC[zz, y, :, self.head].astype(F32) + self.RY[zz].astype(F32)
            ).astype(BF)
            self.add_beyond(chunk, self.ZA, 16, below, zz)
            self.pass_on(chunk, self.ZA, 12, 16, below, zz, h)

        self.targets(h, one)

    def pairs_along_z(self, h):
        d, s, z, y, c = place()

        def one(below, zz):
            chunk = self.P.at[zz, :, c, :, self.rest]
            chunk[...] = (chunk[...].astype(F32) + self.RC[zz, :, :, self.rest].astype(F32)).astype(BF)
            self.add_beyond(chunk, self.ZB, 25, below, zz)
            self.pass_on(chunk, self.ZB, 21, 25, below, zz, h)

        self.targets(h, one)

    def pairs_over_y(self):
        d, s, z, y, c = place()
        chunk = self.P.at[z, :, c, :, self.rest]
        chunk[...] = (chunk[...].astype(F32) + self.RC[z, :, :, self.rest].astype(F32)).astype(BF)

        @pl.when(z < 3)
        def _():
            await_bytes(self.ZB.at[z], self.sem.at[25 + z])
            chunk[...] = (chunk[...].astype(F32) + self.ZB[z].astype(F32)).astype(BF)

        @pl.when(z > 0)
        def _():
            await_bytes(self.ZB.at[4], self.sem.at[29])
            chunk[...] = (chunk[...].astype(F32) + self.ZB[4].astype(F32)).astype(BF)

        other = self.P.at[z, 1 - y, c, :, self.rest]
        send(other, self.YB, self.sem.at[30], self.sem.at[31], (d, seq_of(z, 1 - y, c)))

    def total(self):
        d, s, z, y, c = place()
        await_bytes(self.RY.at[z], self.sem.at[8 + z])
        head, rest = self.head, self.rest
        self.TOT[:, head] = (
            self.P[z, y, c, :, head].astype(F32) + self.RC[z, y, :, head].astype(F32) + self.RY[z].astype(F32)
        )

        @pl.when(z < 3)
        def _():
            await_bytes(self.ZA.at[z], self.sem.at[16 + z])
            self.TOT[:, head] += self.ZA[z].astype(F32)

        @pl.when(z > 0)
        def _():
            await_bytes(self.ZA.at[4], self.sem.at[20])
            self.TOT[:, head] += self.ZA[4].astype(F32)

        await_bytes(self.YB, self.sem.at[31])
        self.TOT[:, rest] = self.P[z, y, c, :, rest].astype(F32) + self.YB[...].astype(F32)
        return self.TOT[...]

    def release(self):
        d, s, z, y, c = place()
        signal(self.free.at[0], (d, seq_of(z, y, 1 - c)))
        signal(self.free.at[1], (d, seq_of(z, 1 - y, c)))

        @pl.when(z < 3)
        def _():
            signal(self.free.at[3], (d, s + 4))

        @pl.when(z > 0)
        def _():
            signal(self.free.at[2], (d, s - 4))

    def drain(self):
        d, s, z, y, c = place()
        for k in range(2):
            await_bytes(self.RC.at[:, 0], self.sem.at[k])
        for zz in range(4):
            await_bytes(self.RY.at[0], self.sem.at[4 + zz])

            @pl.when(z != zz)
            def _():
                await_bytes(self.ZA.at[0], self.sem.at[12 + zz])
                await_bytes(self.ZB.at[0], self.sem.at[21 + zz])

        await_bytes(self.YB, self.sem.at[30])


def everyone(act):
    d, s, z, y, c = place()

    def one(k, carry):
        other = lax.rem(d * 16 + s + k, 32)
        act((other // 16, other % 16), other)
        return carry

    lax.fori_loop(1, 32, one, 0)


def greet_all():
    barrier = pltpu.get_barrier_semaphore()
    everyone(lambda device, slot: signal(barrier, device))
    pl.semaphore_wait(barrier, 31)


class Exchange:
    def __init__(self, src, dst, ss, rs, same):
        self.src, self.dst, self.ss, self.rs, self.same = src, dst, ss, rs, same

    def start(self):
        d, s, z, y, c = place()
        me = d * 16 + s

        def one(device, slot):
            src = self.src if self.same else self.src.at[slot]
            send(src, self.dst.at[me], self.ss.at[0], self.rs.at[0], device)

        everyone(one)

    def arrived(self):
        await_bytes(self.dst.at[pl.ds(0, 31)], self.rs.at[0])

    def drain(self):
        await_bytes(self.dst.at[pl.ds(0, 31)], self.ss.at[0])


QB = 256


def dot_nt(left, right):
    return lax.dot_general(left, right, (((1,), (1,)), ((), ())), preferred_element_type=F32)


def dot_nn(left, right):
    return jnp.dot(left, right, preferred_element_type=F32)


def head_lanes(shape, dim):
    return lax.broadcasted_iota(jnp.int32, shape, dim) // HEAD


def swap_halves(rows):
    lane = lax.broadcasted_iota(jnp.int32, rows.shape, 1) % HEAD
    return jnp.where(lane < ROT // 2, pltpu.roll(rows, 128 - ROT // 2, 1), pltpu.roll(rows, ROT // 2, 1))


def front_tile(R, m, zt):
    width = R.N.shape[-1]
    n = R.N[m, zt].reshape(QB, width)
    rows = pl.ds(pl.multiple_of(zt * QB, QB), QB)
    merged = dot_nt(n, R.Wq[...].reshape(384, width)) + R.bq[...]
    cos, sin = R.cos[rows, :], R.sin[rows, :]
    query, key, value = merged[:, :128], merged[:, 128:256], merged[:, 256:]
    query = (query * cos + swap_halves(query) * sin).astype(BF)
    key = (key * cos + swap_halves(key) * sin).astype(BF)
    value = value.astype(BF)
    R.Q[rows, :] = query * jnp.asarray(0.125, BF)
    R.K[rows, :] = key
    R.V[rows, :] = value
    R.KT[zt] = key.T
    R.VT[zt] = value.T
    gm = dot_nt(R.DY[m, zt].reshape(QB, width), R.Wd[...].reshape(128, width)).astype(BF)
    R.GM[rows, :] = gm


def hidden_tile(R, m, zt):
    width = R.N.shape[-1]
    rows = pl.ds(pl.multiple_of(zt * QB, QB), QB)
    pre = dot_nt(R.N[m, zt].reshape(QB, width), R.W1[...].reshape(512, width)) + R.b1[...]
    grad = dot_nt(R.DY[m, zt].reshape(QB, width), R.W2[...].reshape(512, width))
    square = pre * pre
    turn = jnp.tanh(TANH_FACTOR * (pre + CUBIC_FACTOR * square * pre))
    half = 0.5 + 0.5 * turn
    slope = half + (0.5 * TANH_FACTOR) * pre * (1.0 - turn * turn) * (1.0 + 3.0 * CUBIC_FACTOR * square)
    R.ACT[m, rows, :] = (pre * half).astype(BF)
    gh = (slope * grad).astype(BF)
    R.GH[m, rows, :] = gh
    R.gh_sum[...] += jnp.sum(gh.astype(F32), 0, keepdims=True)


def attention_tile(R, m, qb, limit):
    (attention_wide if qb < 3 else attention_tall)(R, m, qb, limit)


def attention_wide(R, m, qb, limit):
    chunks = max(2, qb + 1)
    ext = chunks * QB
    q_rows = slice(qb * QB, (qb + 1) * QB)
    zero = jnp.asarray(0, BF)
    lane_head = head_lanes((QB, 128), 1)
    q0, gm0 = R.Q[q_rows, :], R.GM[q_rows, :]
    q = jnp.concatenate([jnp.where(lane_head == h, q0, zero) for h in range(2)], 0)
    gm = jnp.concatenate([jnp.where(lane_head == h, gm0, zero) for h in range(2)], 0)
    reach = jnp.maximum(qb * QB + lax.broadcasted_iota(jnp.int32, (1, 2 * QB), 1) % QB, limit - 1)
    s = dot_nt(R.K[:ext, :], q)
    parts = []
    for kc in range(chunks):
        part = s[kc * QB : (kc + 1) * QB]
        if kc >= qb:
            place_j = kc * QB + lax.broadcasted_iota(jnp.int32, (QB, 2 * QB), 0)
            part = jnp.where(place_j <= reach, part, MASKED_LOW)
        parts.append(part)
    s = jnp.concatenate(parts, 0)
    top = jnp.max(s, 0, keepdims=True)
    e = jnp.exp(s - top)
    total = jnp.sum(e, 0, keepdims=True)
    inverse = 1.0 / total
    eb = e.astype(BF)
    mix = None
    for kc in range(chunks):
        term = dot_nn(R.VT[kc], eb[kc * QB : (kc + 1) * QB])
        mix = term if mix is None else mix + term
    mix = mix * inverse
    row_head = head_lanes((128, 2 * QB), 0)
    lane_block = lax.broadcasted_iota(jnp.int32, (128, 2 * QB), 1) // QB
    own = row_head == lane_block
    gm_t = gm0.astype(F32).T
    gm_t = jnp.concatenate([gm_t, gm_t], 1)
    delta = jnp.sum(jnp.where(own, gm_t * mix, 0.0), 0, keepdims=True)
    p = e * inverse
    gp = dot_nt(R.V[:ext, :], gm)
    ds = (p * (gp - delta)).astype(BF)
    dq = None
    for kc in range(chunks):
        term = dot_nn(R.KT[kc], ds[kc * QB : (kc + 1) * QB])
        dq = term if dq is None else dq + term
    dk = dot_nn(ds, q)
    dv = dot_nn(p.astype(BF), gm)
    done = 0 if qb == 0 else max(2, qb) * QB
    if done:
        R.DK[:done, :] += dk[:done]
        R.DV[:done, :] += dv[:done]
    if done < ext:
        R.DK[done:ext, :] = dk[done:]
        R.DV[done:ext, :] = dv[done:]
    mixed_t = jnp.where(row_head[:, :QB] == 0, mix[:, :QB], mix[:, QB:])
    dq_t = jnp.where(row_head[:, :QB] == 0, dq[:, :QB], dq[:, QB:])
    R.MM[m, q_rows, 384:] = mixed_t.T.astype(BF)
    grad_query = dq_t.T * 0.125
    cos, sin = R.cos[q_rows, :], R.sin[q_rows, :]
    grad_query = (grad_query * cos - swap_halves(grad_query) * sin).astype(BF)
    R.MM[m, q_rows, :128] = grad_query
    R.mm_sum[:, :128] += jnp.sum(grad_query.astype(F32), 0, keepdims=True)


def attention_tall(R, m, qb, limit):
    chunks = max(2, qb + 1)
    ext = chunks * QB
    q_rows = slice(qb * QB, (qb + 1) * QB)
    zero = jnp.asarray(0, BF)
    lane_head = head_lanes((QB, 128), 1)
    row_head = head_lanes((128, QB), 0)
    reach = jnp.maximum(qb * QB + lax.broadcasted_iota(jnp.int32, (1, QB), 1), limit - 1)
    mixed_t, dq_t = [], []
    done = max(2, qb) * QB
    gm_t = R.GM[q_rows, :].astype(F32).T
    for h in range(2):
        q = jnp.where(lane_head == h, R.Q[q_rows, :], zero)
        gm = jnp.where(lane_head == h, R.GM[q_rows, :], zero)
        s = dot_nt(R.K[:ext, :], q)
        parts = []
        for kc in range(chunks):
            part = s[kc * QB : (kc + 1) * QB]
            if kc >= qb:
                place_j = kc * QB + lax.broadcasted_iota(jnp.int32, (QB, QB), 0)
                part = jnp.where(place_j <= reach, part, MASKED_LOW)
            parts.append(part)
        s = jnp.concatenate(parts, 0)
        gp = dot_nt(R.V[:ext, :], gm)
        top = jnp.max(s, 0, keepdims=True)
        e = jnp.exp(s - top)
        total = jnp.sum(e, 0, keepdims=True)
        inverse = 1.0 / total
        eb = e.astype(BF)
        mix = None
        for kc in range(chunks):
            term = dot_nn(R.VT[kc], eb[kc * QB : (kc + 1) * QB])
            mix = term if mix is None else mix + term
        mix = mix * inverse
        delta = jnp.sum(jnp.where(row_head == h, gm_t * mix, 0.0), 0, keepdims=True)
        p = e * inverse
        ds = (p * (gp - delta)).astype(BF)
        dq = None
        for kc in range(chunks):
            term = dot_nn(R.KT[kc], ds[kc * QB : (kc + 1) * QB])
            dq = term if dq is None else dq + term
        dk, dv = dot_nn(ds, q), dot_nn(p.astype(BF), gm)
        fresh = 0 if h else ext - done
        R.DK[: ext - fresh, :] += dk[: ext - fresh]
        R.DV[: ext - fresh, :] += dv[: ext - fresh]
        if fresh:
            R.DK[done:ext, :] = dk[done:]
            R.DV[done:ext, :] = dv[done:]
        mixed_t.append(mix)
        dq_t.append(dq)
    R.MM[m, q_rows, 384:] = jnp.where(row_head == 0, mixed_t[0], mixed_t[1]).T.astype(BF)
    grad_query = jnp.where(row_head == 0, dq_t[0], dq_t[1]).T * 0.125
    cos, sin = R.cos[q_rows, :], R.sin[q_rows, :]
    grad_query = (grad_query * cos - swap_halves(grad_query) * sin).astype(BF)
    R.MM[m, q_rows, :128] = grad_query
    R.mm_sum[:, :128] += jnp.sum(grad_query.astype(F32), 0, keepdims=True)


def key_tile(R, m, i):
    rows = pl.ds(pl.multiple_of(i * QB, QB), QB)
    grad_key = R.DK[rows, :]
    cos, sin = R.cos[rows, :], R.sin[rows, :]
    grad_key = (grad_key * cos - swap_halves(grad_key) * sin).astype(BF)
    grad_value = R.DV[rows, :].astype(BF)
    R.MM[m, rows, 128:256] = grad_key
    R.MM[m, rows, 256:384] = grad_value
    R.mm_sum[:, 128:256] += jnp.sum(grad_key.astype(F32), 0, keepdims=True)
    R.mm_sum[:, 256:384] += jnp.sum(grad_value.astype(F32), 0, keepdims=True)


def out_tile(R, m, i, P):
    rows = pl.ds(pl.multiple_of(i * QB, QB), QB)
    width = R.N.shape[-1]
    mixed = R.MM[m, rows, 384:]
    act = R.ACT[m, rows, :]
    for col in range(0, width, 512):
        cols = slice(col, col + 512)
        total = dot_nn(mixed, R.Wd[:, :, cols].reshape(128, 512)) + dot_nn(act, R.W2[:, :, cols].reshape(512, 512))
        P[i, :, :, :, cols] = total.astype(BF).reshape(2, 2, 64, 512)


def grad_tile(R, m, i, P):
    rows = pl.ds(pl.multiple_of(i * QB, QB), QB)
    width = R.N.shape[-1]
    merged = R.MM[m, rows, :384]
    gh = R.GH[m, rows, :]
    for col in range(0, width, 512):
        cols = slice(col, col + 512)
        total = dot_nn(merged, R.Wq[:, :, cols].reshape(384, 512)) + dot_nn(gh, R.W1[:, :, cols].reshape(512, 512))
        P[i, :, :, :, cols] = total.astype(BF).reshape(2, 2, 64, 512)


def turn_tile(R, src, m, i):
    place_i = (m * 4 + i) * QB
    R.AT[:, place_i : place_i + QB] = src[m, i * QB : (i + 1) * QB, :].T


D0, D1, N0, N1, G0, G1, O0, O1 = range(8)
REST, FIRST, PAIRS, OWN, OTHER, HOP, PAIR_HOP, CORES, OVER_Y, ALONG_Z, PAIRS_Z, PAIRS_Y, TOTAL = range(13)
QKV, OWNERS = (-1, 0, 0), (-2, 0, 0)
(
    AT_GREETED, AT_LOADED, AT_NORM, AT_BEGUN, AT_FRONT0, AT_ATT0, AT_ATT1, AT_HID0, AT_GRAD0, AT_OUT0, AT_FIRST, AT_HID1, AT_W2, AT_FRONT1, AT_WA, AT_GRAD1, AT_THIRD, AT_OUT1, AT_W1, AT_LAST, AT_TAIL,
) = range(21)
PLAN = {
    (AT_NORM, 0): [(D0, REST, 0), (D1, FIRST, 0), (D0, PAIRS, 0), (D1, REST, 0), (D0, FIRST, 0), (N0, REST, 0), (N0, FIRST, 0), (D0, PAIR_HOP, 1), (N0, PAIRS, 0)],
    (AT_BEGUN, 0): [(D0, HOP, 1), (N0, HOP, 1), QKV, (N1, REST, 0), (N0, PAIR_HOP, 1), (D0, HOP, 2), (N0, HOP, 2), (N1, PAIRS, 0), (D0, PAIR_HOP, 2), (N1, PAIR_HOP, 1), (D0, HOP, 3), (N1, PAIR_HOP, 2), (N0, HOP, 3), (D1, HOP, 1), (D0, PAIR_HOP, 3), (N0, PAIR_HOP, 2), (N0, PAIR_HOP, 3), (N0, OWN, 0), (D0, OTHER, 0), (D0, OWN, 0), (D1, PAIRS, 0), (D1, HOP, 2), (N0, OTHER, 0)],
    (AT_FRONT0, 0): [(N1, PAIR_HOP, 3), (D1, HOP, 3), (D1, PAIR_HOP, 1)],
    (AT_FRONT0, 3): [(D1, PAIR_HOP, 2)],
    (AT_ATT0, 1): [(N1, FIRST, 0)],
    (AT_HID0, 2): [(N1, HOP, 1)],
    (AT_HID0, 3): [(D1, PAIR_HOP, 3)],
    (AT_GRAD0, 0): [(N1, HOP, 2)],
    (AT_GRAD0, 1): [(D1, OWN, 0)],
    (AT_GRAD0, 3): [(D1, OTHER, 0), (N1, HOP, 3)],
    (AT_OUT0, 0): [(N1, OWN, 0)],
    (AT_OUT0, 2): [(N1, OTHER, 0), (G0, CORES, 0), (G0, OVER_Y, 3), (G0, PAIRS_Z, 3)],
    (AT_FIRST, 0): [(G0, OVER_Y, 2)],
    (AT_HID1, 0): [(G0, OVER_Y, 1)],
    (AT_HID1, 3): [(O0, CORES, 0), (G0, ALONG_Z, 3), (O0, OVER_Y, 1)],
    (AT_W2, 0): [(G0, PAIRS_Z, 2)],
    (AT_W2, 1): [(G0, ALONG_Z, 2), (O0, OVER_Y, 3)],
    (AT_FRONT1, 0): [(G0, PAIRS_Z, 1)],
    (AT_FRONT1, 2): [(O0, PAIRS_Z, 3), (O0, OVER_Y, 2)],
    (AT_ATT1, 0): [(O0, ALONG_Z, 3)],
    (AT_ATT1, 1): [(G0, PAIRS_Y, 0)],
    (AT_ATT1, 3): [(G0, ALONG_Z, 1), (G0, OVER_Y, 0)],
    (AT_WA, 0): [(O0, ALONG_Z, 2)],
    (AT_WA, 1): [(O0, PAIRS_Z, 2)],
    (AT_WA, 3): [(G0, TOTAL, 0)],
    (AT_GRAD1, 0): [(O0, PAIRS_Z, 1)],
    (AT_THIRD, 0): [(O0, OVER_Y, 0), (O0, ALONG_Z, 1), (O0, PAIRS_Y, 0), (G1, CORES, 0), (G1, OVER_Y, 2), (G1, PAIRS_Z, 3), (G1, PAIRS_Z, 2), (O0, TOTAL, 0)],
    (AT_OUT1, 0): [OWNERS],
    (AT_OUT1, 3): [(G1, OVER_Y, 3)],
    (AT_W1, 0): [(G1, OVER_Y, 0), (G1, ALONG_Z, 3), (G1, PAIRS_Z, 1), (O1, CORES, 0), (O1, OVER_Y, 3)],
    (AT_W1, 2): [(O1, OVER_Y, 2), (G1, ALONG_Z, 2), (G1, OVER_Y, 1)],
    (AT_W1, 3): [(O1, PAIRS_Z, 3), (O1, PAIRS_Z, 2)],
    (AT_LAST, 0): [(O1, OVER_Y, 1), (O1, ALONG_Z, 3), (O1, OVER_Y, 0), (G1, ALONG_Z, 1), (G1, PAIRS_Y, 0), (O1, PAIRS_Z, 1), (O1, ALONG_Z, 2)],
    (AT_TAIL, 0): [(O1, ALONG_Z, 1), (O1, PAIRS_Y, 0)],
}


def loop(count, tile, at=None, name=None):
    def body(i, carry):
        tile(i)
        for k in range(count):
            if at is not None and (name, k) in PLAN:

                @pl.when(i == k)
                def _():
                    at(name, k)

        return carry

    lax.fori_loop(0, count, body, 0)


def layer_kernel(names, *refs):
    R = SimpleNamespace(**dict(zip(names, refs)))
    width = R.N.shape[-1]
    d, s, z, y, c = place()
    me = d * 16 + s
    partner = (1 - d, s)

    loads = [
        pltpu.make_async_copy(R.x_in, R.x, R.load.at[0]),
        pltpu.make_async_copy(R.dy_in.at[0], R.DY.at[0, z, y, c], R.load.at[1]),
        pltpu.make_async_copy(R.dy_in.at[1], R.DY.at[1, z, y, c], R.load.at[2]),
        pltpu.make_async_copy(R.w1_in, R.W1.at[0], R.load.at[3]),
        pltpu.make_async_copy(R.w2_in, R.W2.at[0], R.load.at[4]),
        pltpu.make_async_copy(R.wd_in, R.Wd.at[d], R.load.at[5]),
    ]
    for copy in loads:
        copy.start()

    cut, cut_out = width * 15 // 16, R.RY.shape[-1]
    D = [Gather(R.dy_in.at[m], R.DY.at[m], R.gather_sem.at[0, m], cut) for m in range(2)]
    N = [Gather(R.N.at[m, z, y, c], R.N.at[m], R.gather_sem.at[1, m], cut) for m in range(2)]

    def scatter(t, m):
        bufs = [R.RC.at[t], R.RY.at[t], R.ZA.at[t], R.ZB.at[t], R.YB.at[t], R.TOT]
        return Scatter((R.PA, R.PB)[t], *bufs, R.scatter_sem.at[t, m], R.free.at[t], m == 1, cut_out)

    O = [scatter(0, m) for m in range(2)]
    G = [scatter(1, m) for m in range(2)]
    small = Exchange(R.pack, R.SG, R.ps, R.pr, True)
    sums = Exchange(R.SG, R.RT, R.ts, R.tr, False)

    steps = {}
    for name, job in ((D0, D[0]), (D1, D[1]), (N0, N[0]), (N1, N[1])):
        for key, step in (
            (REST, job.start_rest), (FIRST, job.start_first), (PAIRS, job.pairs), (OWN, job.own_line), (OTHER, job.other_line),
        ):
            steps[name, key, 0] = step
        for h in (1, 2, 3):
            steps[name, HOP, h] = partial(job.hop, h)
            steps[name, PAIR_HOP, h] = partial(job.pair_hop, h)
    for name, job in ((O0, O[0]), (O1, O[1]), (G0, G[0]), (G1, G[1])):
        steps[name, CORES, 0] = job.cores
        steps[name, PAIRS_Y, 0] = job.pairs_over_y
        for h in (0, 1, 2, 3):
            steps[name, OVER_Y, h] = partial(job.over_y, h)
            steps[name, ALONG_Z, h] = partial(job.along_z, h)
            steps[name, PAIRS_Z, h] = partial(job.pairs_along_z, h)

    def forward_qkv():
        for i in range(3):
            await_bytes(R.Wq.at[3 * d + i], R.qr.at[3 * d + i])
        mine = R.Wq.at[pl.ds(3 * d, 3)]
        send(mine, mine, R.ws.at[3], R.wr.at[3], partner)
        send(R.w1_in, R.W1.at[1], R.ws.at[2], R.wr.at[2], partner)

    steps[QKV] = forward_qkv

    def do(*names):
        for name in names:
            steps[name]()

    def at(place_name, k=0):
        do(*PLAN.get((place_name, k), ()))

    greet_all()
    at(AT_GREETED)
    small.start()
    for i in range(3):
        b = me * 3 + i
        target, entry = b % 16, b // 16

        @pl.when(target == s)
        def _():
            local(R.wq_in.at[i], R.Wq.at[entry], R.qr.at[entry])

        @pl.when(target != s)
        def _():
            send(R.wq_in.at[i], R.Wq.at[entry], R.qs.at[i], R.qr.at[entry], (d, target))

    send(R.wd_in, R.Wd.at[d], R.ws.at[0], R.wr.at[0], partner)
    send(R.w2_in, R.W2.at[1], R.ws.at[1], R.wr.at[1], partner)
    loads[1].wait()
    loads[2].wait()
    at(AT_LOADED)

    R.SG[me] = R.pack[...]
    loads[0].wait()
    small.arrived()
    for j in range(width // 128):
        R.GV[:, 128 * j : 128 * j + 128] = R.SG[2 * j] + R.SG[2 * j + 1]
    gain, shift = R.GV[0:1, :], R.GV[1:2, :]
    for m in range(2):
        rows = R.x[m].astype(F32)
        centred = rows - jnp.mean(rows, 1, keepdims=True)
        rstd = lax.rsqrt(jnp.mean(centred * centred, 1, keepdims=True) + NORM_EPS)
        R.N[m, z, y, c] = (centred * rstd * gain + shift).astype(BF)
        at(AT_NORM, m)
    for p in range(3):
        row = None
        for e in range(2):
            b = s + 16 * (2 * p + e)
            part = R.SG[b // 3, pl.ds(3 + b % 3, 1), :]
            row = part if row is None else row + part
        R.bq[:, 128 * p : 128 * p + 128] = row
    for k in range(2):
        R.b1[:, 128 * k : 128 * k + 128] = R.SG[me, 6 + k : 7 + k, :]
        R.b1[:, 256 + 128 * k : 384 + 128 * k] = R.SG[(1 - d) * 16 + s, 6 + k : 7 + k, :]
    R.gh_sum[...] = jnp.zeros_like(R.gh_sum)
    R.mm_sum[...] = jnp.zeros_like(R.mm_sum)
    R.row_sums[...] = jnp.zeros_like(R.row_sums)

    at(AT_BEGUN)

    D[0].arrived()
    N[0].arrived()
    for copy in loads[3:]:
        copy.wait()
    await_bytes(R.Wd.at[0], R.wr.at[0])
    await_bytes(R.Wq.at[pl.ds(0, 3)], R.wr.at[3])

    def turn(src):
        for m in range(2):
            for i in range(4):
                turn_tile(R, src, m, i)

    stages = [R.stage.at[0], R.stage.at[1]]
    pending = [None, None]

    def keep(value, rows, cols, k):
        if pending[k % 2] is not None:
            pending[k % 2].wait()
        stage = stages[k % 2].at[: value.shape[0], :]
        stage[...] = value
        pending[k % 2] = pltpu.make_async_copy(stage, R.own.at[rows, cols], R.stage_sem.at[k % 2])
        pending[k % 2].start()

    def keep_both(value, lo, cols):
        keep(value[:128], slice(lo, lo + 128), cols, 0)
        keep(value[128:], slice(lo + 128, lo + 256), cols, 1)

    def hidden_grads(src, tokens, lo, sem, name):
        turn(src)
        for k, col in enumerate(range(0, width, 512)):
            cols = slice(col, col + 512)
            total = dot_nn(R.AT[...], tokens[:, :, :, :, :, cols].reshape(8 * QB, 512))
            keep_both(total[:256], lo, cols)
            R.gx[lo : lo + 256, cols] = total[256:].astype(BF)
            at(name, k)
        rows = slice(lo, lo + 256)
        send(R.gx.at[rows], R.RX.at[rows], R.xs.at[sem], R.xr.at[sem], partner)

    def attention_grads():
        turn(R.MM)
        for k, col in enumerate(range(0, width, 512)):
            cols = slice(col, col + 512)
            gq = dot_nn(R.AT[:384, :], R.N[:, :, :, :, :, cols].reshape(8 * QB, 512))
            R.gq[:, :, cols] = gq.astype(BF).reshape(6, 64, 512)
            gd = dot_nn(R.AT[384:, :], R.DY[:, :, :, :, :, cols].reshape(8 * QB, 512))
            keep(jnp.where(d == 0, gd[:64], gd[64:]), slice(512, 576), cols, k)
            R.gx[512:, cols] = jnp.where(d == 0, gd[64:], gd[:64]).astype(BF)
            at(AT_WA, k)
        send(R.gq.at[pl.ds(3 * (1 - d), 3)], R.XB, R.xs.at[0], R.xr.at[0], partner)
        send(R.gx.at[512:], R.RX.at[512:], R.xs.at[1], R.xr.at[1], partner)

    def attention(m):
        limit = R.limits[m : m + 1, :]
        for qb in range(4):
            attention_tile(R, m, qb, limit)
            at((AT_ATT0, AT_ATT1)[m], qb)
        loop(4, partial(key_tile, R, m))

    def finish_out(m):
        total = O[m].total()
        R.hidden_out[m] = (R.x[m].astype(F32) + total + R.GV[2:3, :]).astype(BF)
        if m == 0:
            O[m].release()

    def finish_grad(m):
        total = G[m].total()
        rows = R.x[m].astype(F32)
        centred = rows - jnp.mean(rows, 1, keepdims=True)
        rstd = lax.rsqrt(jnp.mean(centred * centred, 1, keepdims=True) + NORM_EPS)
        xhat = centred * rstd
        g = total * R.GV[0:1, :]
        dy = R.DY[m, z, y, c].astype(F32)
        R.input_grad[m] = dy + rstd * (g - jnp.mean(g, 1, keepdims=True) - xhat * jnp.mean(g * xhat, 1, keepdims=True))
        R.row_sums[0:1, :] += jnp.sum(total * xhat, 0, keepdims=True)
        R.row_sums[1:2, :] += jnp.sum(total, 0, keepdims=True)
        R.row_sums[2:3, :] += jnp.sum(dy, 0, keepdims=True)
        if m == 0:
            G[m].release()

    def to_owners():
        await_bytes(R.XB, R.xr.at[0])
        await_bytes(R.XB, R.xs.at[0])
        for i in range(3):
            b = s + 16 * (3 * d + i)
            owner, where = b // 3 - 16 * d, b % 3
            block = R.gq.at[3 * d + i]
            block[...] = (block[...].astype(F32) + R.XB[i].astype(F32)).astype(BF)

            @pl.when(owner == s)
            def _():
                local(block, R.RQ.at[where], R.rqr.at[where])

            @pl.when(owner != s)
            def _():
                send(block, R.RQ.at[where], R.rqs.at[i], R.rqr.at[where], (d, owner))

    steps.update({(G0, TOTAL, 0): partial(finish_grad, 0), (O0, TOTAL, 0): partial(finish_out, 0), OWNERS: to_owners})
    loop(4, partial(front_tile, R, 0), at, AT_FRONT0)
    attention(0)
    await_bytes(R.W2.at[1], R.wr.at[1])
    await_bytes(R.W1.at[1], R.wr.at[2])
    loop(4, partial(hidden_tile, R, 0), at, AT_HID0)
    loop(4, lambda i: grad_tile(R, 0, i, R.PB), at, AT_GRAD0)
    G[0].start()
    loop(4, lambda i: out_tile(R, 0, i, R.PA), at, AT_OUT0)
    O[0].start()
    at(AT_FIRST)
    D[1].arrived()
    N[1].arrived()
    loop(4, partial(hidden_tile, R, 1), at, AT_HID1)
    hidden_grads(R.ACT, R.DY, 0, 2, AT_W2)
    loop(4, partial(front_tile, R, 1), at, AT_FRONT1)
    attention(1)
    attention_grads()
    G[0].drain()
    loop(4, lambda i: grad_tile(R, 1, i, R.PB), at, AT_GRAD1)
    G[1].start()
    at(AT_THIRD)
    O[0].drain()
    loop(4, lambda i: out_tile(R, 1, i, R.PA), at, AT_OUT1)
    O[1].start()
    hidden_grads(R.GH, R.N, 256, 3, AT_W1)
    at(AT_LAST)
    finish_grad(1)
    R.SG[...] = jnp.zeros_like(R.SG)
    for owner in range(32):
        block = slice(128 * (owner // 2), 128 * (owner // 2) + 128)
        R.SG[owner, 0:3, :] = R.row_sums[0:3, block]
    lane_half = head_lanes((1, 128), 1)
    for j in range(6):
        b = s + 16 * j
        row = R.mm_sum[:, 128 * (j // 2) : 128 * (j // 2) + 128]
        R.SG[b // 3, pl.ds(3 + b % 3, 1), :] = jnp.where(lane_half == j % 2, row, 0.0)
    for k in range(2):
        R.SG[me, 6 + k : 7 + k, :] = R.gh_sum[:, 128 * k : 128 * k + 128]
        R.SG[(1 - d) * 16 + s, 6 + k : 7 + k, :] = R.gh_sum[:, 256 + 128 * k : 384 + 128 * k]
    sums.start()
    R.RT[me] = R.SG[me]
    at(AT_TAIL)
    sums.arrived()
    R.small_out[...] = jnp.sum(R.RT[...], 0)
    finish_out(1)

    for i in range(3):
        await_bytes(R.RQ.at[i], R.rqr.at[i])
        b = s + 16 * (3 * d + i)

        @pl.when(b // 3 - 16 * d != s)
        def _():
            await_bytes(R.gq.at[i], R.rqs.at[i])

        @pl.when((me * 3 + i) % 16 != s)
        def _():
            await_bytes(R.wq_in.at[i], R.qs.at[i])

    for k, rows in ((1, slice(512, 576)), (2, slice(0, 256)), (3, slice(256, 512))):
        await_bytes(R.gx.at[rows], R.xs.at[k])
        await_bytes(R.RX.at[rows], R.xr.at[k])
    await_bytes(R.Wd.at[0], R.ws.at[0])
    await_bytes(R.W2.at[0], R.ws.at[1])
    await_bytes(R.W1.at[0], R.ws.at[2])
    await_bytes(R.Wq.at[pl.ds(0, 3)], R.ws.at[3])
    for copy in pending:
        copy.wait()
    for job in D + N + [O[1], G[1], small, sums]:
        job.drain()


def run_layer(pack, x, dy, wq, wd, w1, w2, cos, sin, limits):
    width = x.shape[-1]
    vm = pl.BlockSpec(memory_space=pltpu.VMEM)
    hbm = pl.BlockSpec(memory_space=pl.ANY)
    dma = pltpu.SemaphoreType.DMA
    names = ["pack", "x_in", "dy_in", "wq_in", "wd_in", "w1_in", "w2_in", "cos", "sin", "limits"]
    names += ["hidden_out", "input_grad", "small_out", "own", "RX", "RQ"]

    def low(*shape):
        return pltpu.VMEM(shape, BF)

    def wide(*shape):
        return pltpu.VMEM(shape, F32)

    chunks = (4, 2, 2, 64, width)
    cut = width * 14 // 16
    scratch = dict(
        N=low(2, *chunks), DY=low(2, *chunks), x=low(2, 64, width),
        Wq=low(6, 64, width), Wd=low(2, 64, width), W1=low(2, 256, width), W2=low(2, 256, width),
        SG=wide(32, 8, 128), GV=wide(8, width), bq=wide(1, 384), b1=wide(1, 512),
        Q=low(1024, 128), K=low(1024, 128), V=low(1024, 128), GM=low(1024, 128),
        KT=low(4, 128, QB), VT=low(4, 128, QB),
        ACT=low(2, 1024, 512), GH=low(2, 1024, 512), MM=low(2, 1024, 512), AT=low(512, 2048),
        DK=wide(1024, 128), DV=wide(1024, 128),
        PA=low(*chunks), PB=low(*chunks),
        RC=low(2, 4, 2, 64, width), RY=low(2, 4, 64, cut), ZA=low(2, 5, 64, cut), ZB=low(2, 5, 2, 64, max(128, width - cut)),
        YB=low(2, 64, max(128, width - cut)), TOT=wide(64, width),
        gq=low(6, 64, width), gx=low(576, width), XB=low(3, 64, width), stage=wide(2, 128, 512),
        gh_sum=wide(1, 512), mm_sum=wide(1, 384), row_sums=wide(8, width), RT=wide(32, 8, 128),
        load=dma((6,)), gather_sem=dma((2, 2, Gather.SEMS)), scatter_sem=dma((2, 2, Scatter.SEMS)),
        free=pltpu.SemaphoreType.REGULAR((2, 4)),
        ps=dma((1,)), pr=dma((1,)), ts=dma((1,)), tr=dma((1,)),
        qs=dma((3,)), qr=dma((6,)), ws=dma((4,)), wr=dma((4,)), xs=dma((4,)), xr=dma((4,)), rqs=dma((3,)), rqr=dma((3,)),
        stage_sem=dma((2,)),
    )
    return pl.pallas_call(
        partial(layer_kernel, names + list(scratch)),
        name="layer",
        out_shape=(
            jax.ShapeDtypeStruct((2, 64, width), BF),
            jax.ShapeDtypeStruct((2, 64, width), F32),
            jax.ShapeDtypeStruct((8, 128), F32),
            jax.ShapeDtypeStruct((576, width), F32),
            jax.ShapeDtypeStruct((576, width), BF),
            jax.ShapeDtypeStruct((3, 64, width), BF),
        ),
        in_specs=[vm] + [hbm] * 6 + [vm, vm, vm],
        out_specs=(vm, vm, vm, hbm, hbm, hbm),
        scratch_shapes=list(scratch.values()),
        compiler_params=pltpu.CompilerParams(collective_id=0, has_side_effects=True, vmem_limit_bytes=251 * 2**18),
    )(pack, x, dy, wq.reshape(3, 64, width), wd, w1, w2, cos, sin, limits)


def finish_kernel(own, RX, RQ, hidden_in, input_in, qkv, dense, fc1, fc2, hidden_out, input_grad):
    qkv[...] = RQ[...].reshape(qkv.shape).astype(F32)
    fc2[...] = own[:256, :] + RX[:256, :].astype(F32)
    fc1[...] = own[256:512, :] + RX[256:512, :].astype(F32)
    dense[...] = own[512:, :] + RX[512:, :].astype(F32)
    hidden_out[...] = hidden_in[...]
    input_grad[...] = input_in[...]


def run_finish(own, RX, RQ, hidden_out, input_grad):
    width = own.shape[1]
    part = width // 4

    def rows(count):
        return pl.BlockSpec((count, part), lambda i: (0, i))

    def cube(a, b):
        return pl.BlockSpec((a, b, part), lambda i: (0, 0, i))

    return pl.pallas_call(
        finish_kernel,
        name="finish",
        grid=(4,),
        out_shape=(
            jax.ShapeDtypeStruct((192, width), F32),
            jax.ShapeDtypeStruct((64, width), F32),
            jax.ShapeDtypeStruct((256, width), F32),
            jax.ShapeDtypeStruct((256, width), F32),
            jax.ShapeDtypeStruct(hidden_out.shape, BF),
            jax.ShapeDtypeStruct(input_grad.shape, F32),
        ),
        in_specs=[rows(576), rows(576), cube(3, 64), cube(2, 64), cube(2, 64)],
        out_specs=(rows(192), rows(64), rows(256), rows(256), cube(2, 64), cube(2, 64)),
        compiler_params=pltpu.CompilerParams(vmem_limit_bytes=62 * 2**20),
    )(own, RX, RQ, hidden_out, input_grad)


def rotary_rows(length):
    half_rot = ROT // 2
    frequency = np.power(np.float32(10000.0), -np.arange(half_rot, dtype=np.float32) * np.float32(2.0) / np.float32(ROT))
    angles = np.arange(length, dtype=np.float32)[:, None] * frequency.astype(np.float32)[None, :]
    cosine, sine = np.cos(angles), np.sin(angles)
    rest = np.zeros((length, HEAD - ROT), np.float32)
    cosine = np.concatenate([cosine, cosine, rest + 1.0], 1)
    sine = np.concatenate([-sine, sine, rest], 1)
    return np.tile(cosine, (1, 2)).astype(np.float32), np.tile(sine, (1, 2)).astype(np.float32)


def by_heads(
    hidden_in, cotangent, prefix_len, qkv_weight, dense_weight, fc1_weight, fc2_weight,
    norm_gain, norm_shift, qkv_bias, dense_bias, fc1_bias, fc2_bias,
):
    width = hidden_in.shape[-1]
    d, s, z, y, c = place()
    me = d * 16 + s

    def beside(rows, right):
        right = jnp.reshape(right, (-1, 1))
        return jnp.concatenate([jnp.where(right, 0.0, rows), jnp.where(right, rows, 0.0)], 1)

    both = dense_bias.astype(F32) + fc2_bias.astype(F32)
    thirds = jnp.stack([norm_gain.astype(F32), norm_shift.astype(F32), both])
    pack = jnp.concatenate(
        [
            beside(thirds, me % 2 == 1),
            beside(qkv_bias.astype(F32).reshape(3, 64), ((me * 3 + jnp.arange(3)) // 16) % 2 == 1),
            fc1_bias.astype(F32).reshape(2, 128),
        ],
        0,
    )
    cos, sin = rotary_rows(hidden_in.shape[2] * 16)
    hidden_out, input_grad, small, own, RX, RQ = run_layer(
        pack, hidden_in.reshape(2, 64, width), cotangent.reshape(2, 64, width),
        qkv_weight, dense_weight, fc1_weight, fc2_weight, cos, sin, prefix_len,
    )
    qkv_grad, dense_grad, fc1_grad, fc2_grad, hidden_out, input_grad = run_finish(own, RX, RQ, hidden_out, input_grad)
    thirds = jnp.where(me % 2 == 1, small[:3, 64:], small[:3, :64])
    return (
        hidden_out.reshape(hidden_in.shape),
        input_grad.reshape(hidden_in.shape),
        qkv_grad,
        dense_grad,
        fc1_grad,
        fc2_grad,
        thirds[0],
        thirds[1],
        (small[3:6, :64] + small[3:6, 64:]).reshape(192),
        thirds[2],
        small[6:8].reshape(256),
        thirds[2],
    )


def solution(mesh):
    in_specs = (
        P(None, "dp", "seq", None),
        P(None, "dp", "seq", None),
        P(None, "dp"),
        P(("dp", "seq"), None),
        P(("dp", "seq"), None),
        P(("dp", "seq"), None),
        P(("dp", "seq"), None),
        P(("dp", "seq")),
        P(("dp", "seq")),
        P(("dp", "seq")),
        P(("dp", "seq")),
        P(("dp", "seq")),
        P(("dp", "seq")),
    )
    out_specs = (
        P(None, "dp", "seq", None),
        P(None, "dp", "seq", None),
        P(("dp", "seq"), None),
        P(("dp", "seq"), None),
        P(("dp", "seq"), None),
        P(("dp", "seq"), None),
        P(("dp", "seq")),
        P(("dp", "seq")),
        P(("dp", "seq")),
        P(("dp", "seq")),
        P(("dp", "seq")),
        P(("dp", "seq")),
    )
    fits = mesh.shape["dp"] == 2 and mesh.shape["seq"] == 16

    def body(*args):
        return (by_heads if fits and args[0].shape[0] == 2 and args[0].shape[2] == 64 else on_device)(*args)

    return jax.shard_map(
        body, mesh=mesh, in_specs=in_specs, out_specs=out_specs, check_vma=False
    )
```
